32 devices in a mesh: seq: 8 (over z, y), dp: 4 (over x, core).
Axes of the slice: x: 2, y: 2, z: 4, core: 2. Of those that a mesh axis runs over, the one named last changes fastest.
Arguments:
- signal: bfloat16 [4, 8192, 384], P('dp', 'seq'), may hold values from -6 to 6
- filter_raw: bfloat16 [8192, 384], P('seq'), may hold values from -6 to 6
- cotangent: bfloat16 [4, 8192, 384], P('dp', 'seq'), may hold values from -6 to 6
- block_mask: int32 [4, 8], P('dp', 'seq'), may hold values from 0 to 1, as said below
Outputs:
- conv_out: bfloat16 [4, 8192, 384], P('dp', 'seq')
- signal_grad: bfloat16 [4, 8192, 384], P('dp', 'seq')
- filter_grad: bfloat16 [8192, 384], P('seq')
The draws below stay inside these ranges and needn't reach their ends.
Inputs may be any that keep to these rules, and one draw needn't show every extreme that they name: `block_mask`: each sequence's row is 1 on a leading run of blocks and 0 on the rest; every row has both.
All inputs are finite; a program needn't handle non-finite values.
Results may differ from the reference program's by a relative error of at most 0.013.
Values may be sent and summed in bfloat16 or wider, within the bound.
No kernel may reach another device: no remote copies, remote signals or barrier semaphores. Data moves between devices by JAX's collectives and lax.ppermute only.
A program may use at most 128 MiB of HBM per device.

```python
import math
import jax
import jax.numpy as jnp
from jax import lax

CH = 384
BLK = 1024
RAD = 32
SEQ = 8192
RB = 8
NB = 16
BATCH = 4


def draw_block_mask(key, part):
    counts = jax.random.randint(key, (BATCH,), RB // 2, RB)
    return (jnp.arange(RB)[None, :] < counts[:, None]).astype(jnp.int32)


def steps_of(stream_key, extent, shards, smallest, largest):
    def one(position, shards_of):
        steps = jax.random.uniform(jax.random.fold_in(jax.random.fold_in(stream_key, 6), position), (shards_of,), jnp.float32, smallest / len(shards), largest / len(shards))
        return jnp.repeat(jnp.exp(steps), extent[position] // shards_of).reshape((-1,) + (1,) * (len(extent) - position - 1))

    gain = one(*shards[0])
    for cut in shards[1:]:
        gain = gain * one(*cut)
    return gain


def noise(key, dims, spread, bound, pieces=(), kind=jnp.bfloat16):
    level = steps_of(key, dims, pieces, -0.22, 0.18) if pieces else 1.0
    array = jax.random.normal(key, dims, jnp.float32) * spread * level
    return jnp.minimum(jnp.maximum(array, -bound), bound).astype(kind)


def setup_inputs(seed: int = 0) -> dict:
    streams_of = jax.random.split(jax.random.key(seed), 5)
    return {
        "signal": noise(streams_of[0], (BATCH, SEQ, CH), 1.0, 6.0, ((0, 4), (1, 8))),
        "filter_raw": noise(streams_of[1], (SEQ, CH), 1.0, 6.0, ((0, 8),)),
        "cotangent": noise(streams_of[2], (BATCH, SEQ, CH), 1.0, 6.0, ((0, 4), (1, 8))),
        "block_mask": draw_block_mask(jax.random.fold_in(streams_of[4], 71), 0),
    }


def angle_table(row_ids, col_ids, period):
    product = row_ids[:, None] * col_ids[None, :] % period
    return 2.0 * math.pi / period * product.astype(jnp.float32)

def rounded(values):
    return lax.optimization_barrier(values.astype(jnp.bfloat16)).astype(jnp.float32)

def table_pair(angles):
    return (jnp.cos(angles).astype(jnp.bfloat16).astype(jnp.float32), jnp.sin(angles).astype(jnp.bfloat16).astype(jnp.float32))

def make_tables():
    freq_ids = jnp.arange(NB, dtype=jnp.int32)
    block_ids = jnp.arange(RB, dtype=jnp.int32)
    column_ids = jnp.arange(BLK, dtype=jnp.int32)
    radix_ids = jnp.arange(RAD, dtype=jnp.int32)
    cos_one, sin_one = table_pair(angle_table(freq_ids, block_ids, NB))
    cos_rad, sin_rad = table_pair(angle_table(radix_ids, radix_ids, RAD))
    twist = angle_table(freq_ids, column_ids, NB * BLK)
    inner_twist = angle_table(radix_ids, radix_ids, BLK)
    return (cos_one, sin_one, cos_rad, sin_rad, jnp.cos(twist), jnp.sin(twist), jnp.cos(inner_twist), jnp.sin(inner_twist))

def forward_transform(values, tables):
    cos_one, sin_one, cos_rad, sin_rad, twist_cos, twist_sin, inner_cos, inner_sin = tables
    count = values.shape[0]
    data_rows = values.astype(jnp.float32)
    first_real = jnp.einsum('ka,nab->nkb', cos_one, data_rows)
    first_imag = -jnp.einsum('ka,nab->nkb', sin_one, data_rows)
    turned_real = rounded(first_real * twist_cos + first_imag * twist_sin).reshape(count, NB, RAD, RAD)
    turned_imag = rounded(first_imag * twist_cos - first_real * twist_sin).reshape(count, NB, RAD, RAD)
    mid_real = jnp.einsum('pr,nkpq->nkrq', cos_rad, turned_real) + jnp.einsum('pr,nkpq->nkrq', sin_rad, turned_imag)
    mid_imag = jnp.einsum('pr,nkpq->nkrq', cos_rad, turned_imag) - jnp.einsum('pr,nkpq->nkrq', sin_rad, turned_real)
    spun_real = rounded(mid_real * inner_cos + mid_imag * inner_sin)
    spun_imag = rounded(mid_imag * inner_cos - mid_real * inner_sin)
    last_real = jnp.einsum('qs,nkrq->nksr', cos_rad, spun_real) + jnp.einsum('qs,nkrq->nksr', sin_rad, spun_imag)
    last_imag = jnp.einsum('qs,nkrq->nksr', cos_rad, spun_imag) - jnp.einsum('qs,nkrq->nksr', sin_rad, spun_real)
    return (last_real.reshape(count, NB, BLK), last_imag.reshape(count, NB, BLK))

def inverse_transform(spec_real, spec_imag, factor, tables):
    cos_one, sin_one, cos_rad, sin_rad, twist_cos, twist_sin, inner_cos, inner_sin = tables
    count = spec_real.shape[0]
    round_real = rounded(spec_real).reshape(count, NB, RAD, RAD)
    round_imag = rounded(spec_imag).reshape(count, NB, RAD, RAD)
    mid_real = jnp.einsum('sq,nksr->nkrq', cos_rad, round_real) - jnp.einsum('sq,nksr->nkrq', sin_rad, round_imag)
    mid_imag = jnp.einsum('sq,nksr->nkrq', cos_rad, round_imag) + jnp.einsum('sq,nksr->nkrq', sin_rad, round_real)
    spun_real = rounded(mid_real * inner_cos - mid_imag * inner_sin)
    spun_imag = rounded(mid_imag * inner_cos + mid_real * inner_sin)
    back_real = jnp.einsum('rp,nkrq->nkpq', cos_rad, spun_real) - jnp.einsum('rp,nkrq->nkpq', sin_rad, spun_imag)
    back_imag = jnp.einsum('rp,nkrq->nkpq', cos_rad, spun_imag) + jnp.einsum('rp,nkrq->nkpq', sin_rad, spun_real)
    back_real = back_real.reshape(count, NB, BLK)
    back_imag = back_imag.reshape(count, NB, BLK)
    turned_real = rounded(back_real * twist_cos - back_imag * twist_sin)
    turned_imag = rounded(back_imag * twist_cos + back_real * twist_sin)
    combined = jnp.einsum('ka,nkb->nab', cos_one, turned_real) - jnp.einsum('ka,nkb->nab', sin_one, turned_imag)
    return (combined * factor).astype(jnp.bfloat16)

def reference(signal, filter_raw, cotangent, block_mask):
    tables = make_tables()
    factor = 1.0 / (NB * BLK * math.sqrt(SEQ))
    mask_blocks = block_mask.astype(jnp.bfloat16)[:, :, None]

    def channel(inputs):
        signal_row, filter_row, grad_row = inputs
        masked = signal_row.reshape(BATCH, RB, BLK) * mask_blocks
        signal_real, signal_imag = forward_transform(masked, tables)
        filter_real, filter_imag = forward_transform(filter_row.reshape(1, RB, BLK), tables)
        grad_real, grad_imag = forward_transform(grad_row.reshape(BATCH, RB, BLK), tables)
        out_real = signal_real * filter_real - signal_imag * filter_imag
        out_imag = signal_real * filter_imag + signal_imag * filter_real
        input_real = grad_real * filter_real + grad_imag * filter_imag
        input_imag = grad_imag * filter_real - grad_real * filter_imag
        weight_real = lax.optimization_barrier(jnp.sum(grad_real * signal_real + grad_imag * signal_imag, axis=0, keepdims=True))
        weight_imag = lax.optimization_barrier(jnp.sum(grad_imag * signal_real - grad_real * signal_imag, axis=0, keepdims=True))
        conv_rows = inverse_transform(out_real, out_imag, factor, tables)
        input_rows = inverse_transform(input_real, input_imag, factor, tables) * mask_blocks
        weight_rows = inverse_transform(weight_real, weight_imag, factor, tables)
        return (conv_rows.reshape(BATCH, SEQ), input_rows.reshape(BATCH, SEQ), weight_rows.reshape(SEQ))
    outputs = lax.map(channel, (jnp.transpose(signal, (2, 0, 1)), jnp.transpose(filter_raw, (1, 0)), jnp.transpose(cotangent, (2, 0, 1))))
    return (jnp.transpose(outputs[0], (1, 2, 0)), jnp.transpose(outputs[1], (1, 2, 0)), jnp.transpose(outputs[2], (1, 0)))
```

```python
import functools
import math

import jax
import jax.numpy as jnp
import ml_dtypes
import numpy as np
from jax import lax
from jax.experimental import pallas as pl
from jax.experimental.pallas import tpu as pltpu
from jax.sharding import PartitionSpec as P

LANES = 128
BLK = 1024
BF16 = ml_dtypes.bfloat16


def wave(product, period):
    angle = 2.0 * np.pi / period * (product % period)
    return np.cos(angle), np.sin(angle)


def make_tables(blocks, rows, replicas):
    coarse = blocks * rows
    freq = np.arange(coarse)
    lane = np.arange(LANES)
    own = rows // replicas
    half = rows // 2
    grid_j, grid_r = np.meshgrid(np.arange(blocks), np.arange(rows), indexing="ij")
    plain = grid_j * rows + grid_r
    cos_a, sin_a = wave((4 * freq[:, None] + 1) * np.arange(coarse)[None, :], 4 * coarse)
    first = np.zeros((2, 2, coarse, blocks, 2, rows))
    last = np.zeros((blocks, 2, rows, 2, 2, coarse))
    for which in range(2):
        first[which, 0, :, :, which, :] = cos_a[:, plain]
        first[which, 1, :, :, which, :] = -sin_a[:, plain]
        last[:, which, :, which, 0, :] = np.moveaxis(cos_a[:, plain], 0, 2)
        last[:, which, :, which, 1, :] = -np.moveaxis(sin_a[:, plain], 0, 2)
    taps = (
        np.arange(own)[:, None, None]
        + own * np.arange(replicas)[None, :, None]
        + rows * np.arange(blocks)[None, None, :]
    ).reshape(-1)
    first_taps = np.concatenate([cos_a[:, taps], -sin_a[:, taps]], axis=0)
    back = (
        np.arange(half)[:, None, None]
        + half * np.arange(2)[None, :, None]
        + rows * np.arange(blocks)[None, None, :]
    ).reshape(-1)
    last_taps = np.concatenate([cos_a[:, back], -sin_a[:, back]], axis=0).T
    twist_cos, twist_sin = wave((4 * freq[:, None] + 1) * lane[None, :], 4 * LANES * coarse)
    cos_l, sin_l = wave(lane[:, None] * lane[None, :], LANES)
    inner = np.block([[cos_l, -sin_l], [sin_l, cos_l]])
    inner_back = np.block([[cos_l, sin_l], [-sin_l, cos_l]])
    narrow = (
        first.reshape(4 * coarse, 2 * coarse),
        first_taps,
        inner,
        inner_back,
        last.reshape(2 * coarse, 4 * coarse),
        last_taps,
    )
    return tuple(t.astype(np.float32).astype(BF16) for t in narrow) + (
        twist_cos.astype(np.float32),
        twist_sin.astype(np.float32),
    )


def pack_kernel(own, group, count, mask_ref, signal_ref, grad_ref, filter_ref, send_ref, pair_scr, tap_scr):
    tokens, channels = filter_ref.shape
    rows = tokens // LANES
    pair = 2 * rows
    block_rows = BLK // LANES
    if group * count != channels:
        pair_scr[...] = jnp.zeros_like(pair_scr)
        tap_scr[...] = jnp.zeros_like(tap_scr)
    for row in range(rows):
        span = pl.ds(row * LANES, LANES)
        keep = mask_ref[0, row // block_rows].astype(jnp.float32)
        pair_scr[pl.ds(row, channels, stride=pair), :] = (
            signal_ref[0, span, :].astype(jnp.float32).T * keep
        )
        pair_scr[pl.ds(rows + row, channels, stride=pair), :] = (
            grad_ref[0, span, :].astype(jnp.float32).T
        )
    start = lax.axis_index("dp") * (own * LANES)
    for row in range(own):
        span = pl.ds(pl.multiple_of(start + row * LANES, LANES), LANES)
        tap_scr[pl.ds(row, channels, stride=own), :] = filter_ref[span, :].astype(jnp.float32).T
    for target in range(count):
        send_ref[target, : group * pair, :] = pair_scr[
            target * group * pair : (target + 1) * group * pair, :
        ].astype(jnp.bfloat16)
        send_ref[target, group * pair :, :] = tap_scr[
            target * group * own : (target + 1) * group * own, :
        ].astype(jnp.bfloat16)


def spectral_kernel(
    blocks, rows, replicas, group, factor,
    recv_ref, first_ref, first_taps_ref, inner_ref, inner_back_ref, last_ref, last_taps_ref,
    twist_cos_ref, twist_sin_ref, send_ref, tap_scr, back_scr,
):
    coarse = blocks * rows
    count = blocks * replicas
    pair = 2 * rows
    own = rows // replicas
    half = rows // 2
    tap_rows = group * own
    back_rows = group * half
    for source in range(count):
        tap_scr[source * tap_rows : (source + 1) * tap_rows, :] = recv_ref[
            source, group * pair :, :
        ].astype(jnp.float32)

    def dot(left, right):
        return jnp.dot(left, right, preferred_element_type=jnp.float32)

    def channel(index, carry):
        offset = pl.multiple_of(index * pair, pair)
        twist_cos = twist_cos_ref[...]
        twist_sin = twist_sin_ref[...]

        def turn(real, imag):
            return jnp.concatenate(
                [real * twist_cos + imag * twist_sin, imag * twist_cos - real * twist_sin], axis=1
            ).astype(jnp.bfloat16)

        taps = jnp.concatenate(
            [tap_scr[pl.ds(index * own + row, count, stride=tap_rows), :] for row in range(own)],
            axis=0,
        ).astype(jnp.bfloat16)
        spread_taps = dot(first_taps_ref[...], taps)
        data = jnp.concatenate(
            [
                recv_ref[seq * blocks : (seq + 1) * blocks, pl.ds(offset, pair), :].reshape(
                    blocks * pair, LANES
                )
                for seq in range(replicas)
            ],
            axis=1,
        )
        spread = dot(first_ref[...], data)
        turned = [turn(spread_taps[:coarse], spread_taps[coarse:])]
        for seq in range(replicas):
            part = spread[:, seq * LANES : (seq + 1) * LANES]
            for which in range(2):
                base = 2 * which * coarse
                turned.append(
                    turn(part[base : base + coarse], part[base + coarse : base + 2 * coarse])
                )
        spectrum = dot(jnp.concatenate(turned, axis=0), inner_ref[...])

        def pick(place):
            piece = spectrum[place * coarse : (place + 1) * coarse]
            return piece[:, :LANES], piece[:, LANES:]

        filter_real, filter_imag = pick(0)
        products = []
        weight_real = weight_imag = None
        for seq in range(replicas):
            signal_real, signal_imag = pick(1 + 2 * seq)
            grad_real, grad_imag = pick(2 + 2 * seq)
            out = (
                signal_real * filter_real - signal_imag * filter_imag,
                signal_real * filter_imag + signal_imag * filter_real,
            )
            into = (
                grad_real * filter_real + grad_imag * filter_imag,
                grad_imag * filter_real - grad_real * filter_imag,
            )
            term_real = grad_real * signal_real + grad_imag * signal_imag
            term_imag = grad_imag * signal_real - grad_real * signal_imag
            weight_real = term_real if weight_real is None else weight_real + term_real
            weight_imag = term_imag if weight_imag is None else weight_imag + term_imag
            products.append(jnp.concatenate(out, axis=1).astype(jnp.bfloat16))
            products.append(jnp.concatenate(into, axis=1).astype(jnp.bfloat16))
        products.append(
            jnp.concatenate([weight_real, weight_imag], axis=1).astype(jnp.bfloat16)
        )
        inverted = dot(jnp.concatenate(products, axis=0), inner_back_ref[...])

        def turn_back(place):
            piece = inverted[place * coarse : (place + 1) * coarse]
            real, imag = piece[:, :LANES], piece[:, LANES:]
            return jnp.concatenate(
                [real * twist_cos - imag * twist_sin, imag * twist_cos + real * twist_sin], axis=0
            ).astype(jnp.bfloat16)

        columns = jnp.concatenate(
            [
                jnp.concatenate([turn_back(2 * seq), turn_back(2 * seq + 1)], axis=0)
                for seq in range(replicas)
            ],
            axis=1,
        )
        result = (dot(last_ref[...], columns) * factor).astype(jnp.bfloat16)
        for seq in range(replicas):
            send_ref[seq * blocks : (seq + 1) * blocks, pl.ds(offset, pair), :] = result[
                :, seq * LANES : (seq + 1) * LANES
            ].reshape(blocks, pair, LANES)
        weights = dot(last_taps_ref[...], turn_back(2 * replicas)) * factor
        for row in range(half):
            back_scr[pl.ds(index * half + row, 2 * blocks, stride=back_rows), :] = weights[
                row * 2 * blocks : (row + 1) * 2 * blocks
            ]
        return carry

    lax.fori_loop(0, group, channel, 0)
    for target in range(count):
        place = (target // blocks) % 2 * blocks + target % blocks
        send_ref[target, group * pair :, :] = back_scr[
            place * back_rows : (place + 1) * back_rows, :
        ].astype(jnp.bfloat16)


def unpack_kernel(group, mask_ref, recv_ref, conv_ref, grad_ref, pair_scr):
    tokens, channels = conv_ref.shape[1:]
    rows = tokens // LANES
    pair = 2 * rows
    block_rows = BLK // LANES
    size = group * pair
    for source in range(recv_ref.shape[0]):
        pair_scr[source * size : (source + 1) * size, :] = recv_ref[source, :size, :].astype(
            jnp.float32
        )
    for row in range(rows):
        span = pl.ds(row * LANES, LANES)
        keep = mask_ref[0, row // block_rows].astype(jnp.float32)
        conv_ref[0, span, :] = pair_scr[pl.ds(row, channels, stride=pair), :].T.astype(jnp.bfloat16)
        grad_ref[0, span, :] = (
            pair_scr[pl.ds(rows + row, channels, stride=pair), :].T * keep
        ).astype(jnp.bfloat16)


def unpack_taps_kernel(group, own_ref, other_ref, taps_ref, scr):
    tokens, channels = taps_ref.shape
    half = tokens // LANES // 2
    size = group * half
    side = lax.rem(lax.axis_index("dp"), 2)
    for place, ref in enumerate((own_ref, other_ref)):
        for source in range(ref.shape[0]):
            scr[source * size : (source + 1) * size, :] = ref[source].astype(jnp.float32)
        start = jnp.where(side == place, 0, half * LANES)
        for row in range(half):
            span = pl.ds(pl.multiple_of(start + row * LANES, LANES), LANES)
            taps_ref[span, :] = scr[pl.ds(row, channels, stride=half), :].T.astype(jnp.bfloat16)


VMEM = pl.BlockSpec(memory_space=pltpu.VMEM)
SMEM = pl.BlockSpec(memory_space=pltpu.SMEM)
LIMIT = pltpu.CompilerParams(vmem_limit_bytes=48 * 1024 * 1024)


def per_device(signal, filter_raw, cotangent, block_mask):
    tokens, channels = filter_raw.shape
    blocks = lax.axis_size("seq")
    replicas = lax.axis_size("dp")
    count = blocks * replicas
    group = -(-channels // count)
    rows = tokens // LANES
    pair = 2 * rows
    own = rows // replicas
    half = rows // 2
    total = tokens * blocks
    coarse = total // LANES
    factor = 1.0 / (total * math.sqrt(total))
    everyone = ("dp", "seq")
    tables = [jnp.asarray(t) for t in make_tables(blocks, rows, replicas)]

    packed = pl.pallas_call(
        functools.partial(pack_kernel, own, group, count),
        out_shape=jax.ShapeDtypeStruct((count, group * (pair + own), LANES), jnp.bfloat16),
        in_specs=[SMEM, VMEM, VMEM, VMEM],
        out_specs=VMEM,
        scratch_shapes=[
            pltpu.VMEM((count * group * pair, LANES), jnp.float32),
            pltpu.VMEM((count * group * own, LANES), jnp.float32),
        ],
        compiler_params=LIMIT,
        name="pack",
    )(block_mask, signal, cotangent, filter_raw)
    received = lax.all_to_all(packed, everyone, split_axis=0, concat_axis=0, tiled=True)
    results = pl.pallas_call(
        functools.partial(spectral_kernel, blocks, rows, replicas, group, factor),
        out_shape=jax.ShapeDtypeStruct((count, group * (pair + half), LANES), jnp.bfloat16),
        in_specs=[VMEM] * 9,
        out_specs=VMEM,
        scratch_shapes=[
            pltpu.VMEM((count * group * own, LANES), jnp.float32),
            pltpu.VMEM((2 * blocks * group * half, LANES), jnp.float32),
        ],
        compiler_params=LIMIT,
        name="spectral",
    )(received, *tables)
    returned = lax.all_to_all(results, everyone, split_axis=0, concat_axis=0, tiled=True)
    own_taps = returned[:, group * pair :, :]
    other_taps = lax.ppermute(own_taps, "dp", [(i, i ^ 1) for i in range(replicas)])
    conv_out, signal_grad = pl.pallas_call(
        functools.partial(unpack_kernel, group),
        out_shape=[jax.ShapeDtypeStruct(signal.shape, jnp.bfloat16)] * 2,
        in_specs=[SMEM, VMEM],
        out_specs=[VMEM, VMEM],
        scratch_shapes=[pltpu.VMEM((count * group * pair, LANES), jnp.float32)],
        compiler_params=LIMIT,
        name="unpack",
    )(block_mask, returned)
    filter_grad = pl.pallas_call(
        functools.partial(unpack_taps_kernel, group),
        out_shape=jax.ShapeDtypeStruct(filter_raw.shape, jnp.bfloat16),
        in_specs=[VMEM, VMEM],
        out_specs=VMEM,
        scratch_shapes=[pltpu.VMEM((count * group * half, LANES), jnp.float32)],
        compiler_params=LIMIT,
        name="unpack_taps",
    )(own_taps, other_taps)
    return conv_out, signal_grad, filter_grad


def solution(mesh):
    placed = (P("dp", "seq", None), P("seq", None), P("dp", "seq", None), P("dp", "seq"))
    return jax.shard_map(
        per_device,
        mesh=mesh,
        in_specs=placed,
        out_specs=(P("dp", "seq", None), P("dp", "seq", None), P("seq", None)),
        check_vma=False,
    )
```

```python
import functools
import math

import jax
import jax.numpy as jnp
import ml_dtypes
import numpy as np
from jax import lax
from jax.experimental import pallas as pl
from jax.experimental.pallas import tpu as pltpu
from jax.sharding import PartitionSpec as P

LANES = 128
BLK = 1024
BF16 = ml_dtypes.bfloat16


def wave(product, period):
    angle = 2.0 * np.pi / period * (product % period)
    return np.cos(angle), np.sin(angle)


def make_tables(blocks, rows, replicas):
    coarse = blocks * rows
    freq = np.arange(coarse)
    lane = np.arange(LANES)
    own = rows // replicas
    half = rows // 2
    grid_j, grid_r = np.meshgrid(np.arange(blocks), np.arange(rows), indexing="ij")
    plain = grid_j * rows + grid_r
    cos_a, sin_a = wave((4 * freq[:, None] + 1) * np.arange(coarse)[None, :], 4 * coarse)
    first = np.zeros((2, 2, coarse, blocks, 2, rows))
    last = np.zeros((blocks, 2, rows, 2, 2, coarse))
    for which in range(2):
        first[which, 0, :, :, which, :] = cos_a[:, plain]
        first[which, 1, :, :, which, :] = -sin_a[:, plain]
        last[:, which, :, which, 0, :] = np.moveaxis(cos_a[:, plain], 0, 2)
        last[:, which, :, which, 1, :] = -np.moveaxis(sin_a[:, plain], 0, 2)
    taps = (
        np.arange(own)[:, None, None]
        + rows * np.arange(blocks)[None, :, None]
        + own * np.arange(replicas)[None, None, :]
    ).reshape(-1)
    first_taps = np.concatenate([cos_a[:, taps], -sin_a[:, taps]], axis=0)
    back = (
        np.arange(half)[:, None, None]
        + half * np.arange(2)[None, :, None]
        + rows * np.arange(blocks)[None, None, :]
    ).reshape(-1)
    last_taps = np.concatenate([cos_a[:, back], -sin_a[:, back]], axis=0).T
    twist_cos, twist_sin = wave((4 * freq[:, None] + 1) * lane[None, :], 4 * LANES * coarse)
    cos_l, sin_l = wave(lane[:, None] * lane[None, :], LANES)
    inner = np.block([[cos_l, -sin_l], [sin_l, cos_l]])
    inner_back = np.block([[cos_l, sin_l], [-sin_l, cos_l]])
    narrow = (
        first.reshape(4 * coarse, 2 * coarse),
        first_taps,
        inner,
        inner_back,
        last.reshape(2 * coarse, 4 * coarse),
        last_taps,
    )
    return tuple(t.astype(np.float32).astype(BF16) for t in narrow) + (
        twist_cos.astype(np.float32),
        twist_sin.astype(np.float32),
    )


def pack_kernel(
    own, group, count, mask_ref, signal_ref, grad_ref, filter_ref, send_ref,
    signal_buf, grad_buf, filter_buf, send_buf, pair_scr, tap_scr, in_sems, out_sems,
):
    tokens, channels = filter_ref.shape
    rows = tokens // LANES
    pair = 2 * rows
    block_rows = BLK // LANES
    parts = in_sems.shape[0] // 2
    part_rows = rows // parts
    start = pl.multiple_of(lax.axis_index("dp") * (own * LANES), own * LANES)
    filter_copy = pltpu.make_async_copy(
        filter_ref.at[pl.ds(start, own * LANES), :], filter_buf, in_sems.at[2 * parts]
    )
    copies = []
    for part in range(parts):
        span = pl.ds(part * part_rows * LANES, part_rows * LANES)
        copies.append(
            pltpu.make_async_copy(
                signal_ref.at[0, span, :], signal_buf.at[span, :], in_sems.at[2 * part]
            )
        )
        copies.append(
            pltpu.make_async_copy(
                grad_ref.at[0, span, :], grad_buf.at[span, :], in_sems.at[2 * part + 1]
            )
        )
    filter_copy.start()
    for copy in copies:
        copy.start()
    if group * count != channels:
        pair_scr[...] = jnp.zeros_like(pair_scr)
        tap_scr[...] = jnp.zeros_like(tap_scr)
    filter_copy.wait()
    for row in range(own):
        tap_scr[pl.ds(row, channels, stride=own), :] = (
            filter_buf[row * LANES : (row + 1) * LANES, :].astype(jnp.float32).T
        )
    for part in range(parts):
        places = range(part * part_rows, (part + 1) * part_rows)
        copies[2 * part].wait()
        for row in places:
            keep = mask_ref[0, row // block_rows].astype(jnp.float32)
            pair_scr[pl.ds(row, channels, stride=pair), :] = (
                signal_buf[row * LANES : (row + 1) * LANES, :].astype(jnp.float32).T * keep
            )
        copies[2 * part + 1].wait()
        for row in places:
            pair_scr[pl.ds(rows + row, channels, stride=pair), :] = (
                grad_buf[row * LANES : (row + 1) * LANES, :].astype(jnp.float32).T
            )
    batch = count // out_sems.shape[0]
    sends = []
    for target in range(count):
        send_buf[target, : group * pair, :] = pair_scr[
            target * group * pair : (target + 1) * group * pair, :
        ].astype(jnp.bfloat16)
        send_buf[target, group * pair :, :] = tap_scr[
            target * group * own : (target + 1) * group * own, :
        ].astype(jnp.bfloat16)
        if target % batch == batch - 1:
            span = pl.ds(target + 1 - batch, batch)
            sends.append(
                pltpu.make_async_copy(
                    send_buf.at[span], send_ref.at[span], out_sems.at[target // batch]
                )
            )
            sends[-1].start()
    for copy in sends:
        copy.wait()


def spectral_kernel(
    blocks, rows, replicas, group, factor,
    recv_ref, first_ref, first_taps_ref, inner_ref, inner_back_ref, last_ref, last_taps_ref,
    twist_cos_ref, twist_sin_ref, send_ref, tap_scr, back_scr,
):
    coarse = blocks * rows
    count = blocks * replicas
    pair = 2 * rows
    own = rows // replicas
    half = rows // 2
    tap_rows = group * own
    back_rows = group * half
    for source in range(count):
        tap_scr[source * tap_rows : (source + 1) * tap_rows, :] = recv_ref[
            source, group * pair :, :
        ].astype(jnp.float32)

    def dot(left, right):
        return jnp.dot(left, right, preferred_element_type=jnp.float32)

    def channel(index, carry):
        offset = pl.multiple_of(index * pair, pair)
        twist_cos = twist_cos_ref[...]
        twist_sin = twist_sin_ref[...]

        def turn(real, imag):
            return jnp.concatenate(
                [real * twist_cos + imag * twist_sin, imag * twist_cos - real * twist_sin], axis=1
            ).astype(jnp.bfloat16)

        taps = jnp.concatenate(
            [tap_scr[pl.ds(index * own + row, count, stride=tap_rows), :] for row in range(own)],
            axis=0,
        ).astype(jnp.bfloat16)
        spread_taps = dot(first_taps_ref[...], taps)
        data = jnp.concatenate(
            [
                jnp.concatenate(
                    [
                        recv_ref[block * replicas + seq, pl.ds(offset, pair), :]
                        for block in range(blocks)
                    ],
                    axis=0,
                )
                for seq in range(replicas)
            ],
            axis=1,
        )
        spread = dot(first_ref[...], data)
        turned = [turn(spread_taps[:coarse], spread_taps[coarse:])]
        for seq in range(replicas):
            part = spread[:, seq * LANES : (seq + 1) * LANES]
            for which in range(2):
                base = 2 * which * coarse
                turned.append(
                    turn(part[base : base + coarse], part[base + coarse : base + 2 * coarse])
                )
        spectrum = dot(jnp.concatenate(turned, axis=0), inner_ref[...])

        def pick(place):
            piece = spectrum[place * coarse : (place + 1) * coarse]
            return piece[:, :LANES], piece[:, LANES:]

        filter_real, filter_imag = pick(0)
        products = []
        weight_real = weight_imag = None
        for seq in range(replicas):
            signal_real, signal_imag = pick(1 + 2 * seq)
            grad_real, grad_imag = pick(2 + 2 * seq)
            out = (
                signal_real * filter_real - signal_imag * filter_imag,
                signal_real * filter_imag + signal_imag * filter_real,
            )
            into = (
                grad_real * filter_real + grad_imag * filter_imag,
                grad_imag * filter_real - grad_real * filter_imag,
            )
            term_real = grad_real * signal_real + grad_imag * signal_imag
            term_imag = grad_imag * signal_real - grad_real * signal_imag
            weight_real = term_real if weight_real is None else weight_real + term_real
            weight_imag = term_imag if weight_imag is None else weight_imag + term_imag
            products.append(jnp.concatenate(out, axis=1).astype(jnp.bfloat16))
            products.append(jnp.concatenate(into, axis=1).astype(jnp.bfloat16))
        products.append(
            jnp.concatenate([weight_real, weight_imag], axis=1).astype(jnp.bfloat16)
        )
        inverted = dot(jnp.concatenate(products, axis=0), inner_back_ref[...])

        def turn_back(place):
            piece = inverted[place * coarse : (place + 1) * coarse]
            real, imag = piece[:, :LANES], piece[:, LANES:]
            return jnp.concatenate(
                [real * twist_cos - imag * twist_sin, imag * twist_cos + real * twist_sin], axis=0
            ).astype(jnp.bfloat16)

        columns = jnp.concatenate(
            [
                jnp.concatenate([turn_back(2 * seq), turn_back(2 * seq + 1)], axis=0)
                for seq in range(replicas)
            ],
            axis=1,
        )
        result = (dot(last_ref[...], columns) * factor).astype(jnp.bfloat16)
        for seq in range(replicas):
            for block in range(blocks):
                send_ref[block * replicas + seq, pl.ds(offset, pair), :] = result[
                    block * pair : (block + 1) * pair, seq * LANES : (seq + 1) * LANES
                ]
        weights = dot(last_taps_ref[...], turn_back(2 * replicas)) * factor
        for row in range(half):
            back_scr[pl.ds(index * half + row, 2 * blocks, stride=back_rows), :] = weights[
                row * 2 * blocks : (row + 1) * 2 * blocks
            ]
        return carry

    lax.fori_loop(0, group, channel, 0, unroll=min(group, 12))
    for target in range(count):
        place = target % replicas % 2 * blocks + target // replicas
        send_ref[target, group * pair :, :] = back_scr[
            place * back_rows : (place + 1) * back_rows, :
        ].astype(jnp.bfloat16)


def unpack_kernel(
    group, mask_ref, recv_ref, conv_ref, grad_ref, pair_scr, conv_buf, grad_buf, sems
):
    tokens, channels = conv_ref.shape[1:]
    rows = tokens // LANES
    pair = 2 * rows
    block_rows = BLK // LANES
    size = group * pair
    for source in range(recv_ref.shape[0]):
        pair_scr[source * size : (source + 1) * size, :] = recv_ref[source, :size, :].astype(
            jnp.float32
        )
    copies = []
    for row in range(rows):
        span = pl.ds(row * LANES, LANES)
        keep = mask_ref[0, row // block_rows].astype(jnp.float32)
        conv_buf[span, :] = pair_scr[pl.ds(row, channels, stride=pair), :].T.astype(jnp.bfloat16)
        copies.append(
            pltpu.make_async_copy(conv_buf.at[span, :], conv_ref.at[0, span, :], sems.at[2 * row])
        )
        copies[-1].start()
        grad_buf[span, :] = (
            pair_scr[pl.ds(rows + row, channels, stride=pair), :].T * keep
        ).astype(jnp.bfloat16)
        copies.append(
            pltpu.make_async_copy(
                grad_buf.at[span, :], grad_ref.at[0, span, :], sems.at[2 * row + 1]
            )
        )
        copies[-1].start()
    for copy in copies:
        copy.wait()


def unpack_taps_kernel(group, own_ref, other_ref, taps_ref, scr, taps_buf, sems):
    tokens, channels = taps_ref.shape
    half = tokens // LANES // 2
    size = group * half
    side = lax.rem(lax.axis_index("dp"), 2)
    copies = []
    for place, ref in enumerate((own_ref, other_ref)):
        base = place * ref.shape[0] * size
        for source in range(ref.shape[0]):
            scr[base + source * size : base + (source + 1) * size, :] = ref[source].astype(
                jnp.float32
            )
        start = jnp.where(side == place, 0, half * LANES)
        for row in range(half):
            slot = place * half + row
            span = pl.ds(slot * LANES, LANES)
            taps_buf[span, :] = scr[pl.ds(base + row, channels, stride=half), :].T.astype(
                jnp.bfloat16
            )
            goal = pl.ds(pl.multiple_of(start + row * LANES, LANES), LANES)
            copies.append(
                pltpu.make_async_copy(taps_buf.at[span, :], taps_ref.at[goal, :], sems.at[slot])
            )
            copies[-1].start()
    for copy in copies:
        copy.wait()


VMEM = pl.BlockSpec(memory_space=pltpu.VMEM)
SMEM = pl.BlockSpec(memory_space=pltpu.SMEM)
HBM = pl.BlockSpec(memory_space=pltpu.HBM)
LIMIT = pltpu.CompilerParams(vmem_limit_bytes=48 * 1024 * 1024)


def per_device(signal, filter_raw, cotangent, block_mask):
    tokens, channels = filter_raw.shape
    blocks = lax.axis_size("seq")
    replicas = lax.axis_size("dp")
    count = blocks * replicas
    group = -(-channels // count)
    rows = tokens // LANES
    pair = 2 * rows
    own = rows // replicas
    half = rows // 2
    total = tokens * blocks
    coarse = total // LANES
    factor = 1.0 / (total * math.sqrt(total))
    everyone = ("seq", "dp")
    tables = [jnp.asarray(t) for t in make_tables(blocks, rows, replicas)]

    packed = pl.pallas_call(
        functools.partial(pack_kernel, own, group, count),
        out_shape=jax.ShapeDtypeStruct((count, group * (pair + own), LANES), jnp.bfloat16),
        in_specs=[SMEM, HBM, HBM, HBM],
        out_specs=HBM,
        scratch_shapes=[
            pltpu.VMEM((tokens, channels), jnp.bfloat16),
            pltpu.VMEM((tokens, channels), jnp.bfloat16),
            pltpu.VMEM((own * LANES, channels), jnp.bfloat16),
            pltpu.VMEM((count, group * (pair + own), LANES), jnp.bfloat16),
            pltpu.VMEM((count * group * pair, LANES), jnp.float32),
            pltpu.VMEM((count * group * own, LANES), jnp.float32),
            pltpu.SemaphoreType.DMA((5,)),
            pltpu.SemaphoreType.DMA((4,)),
        ],
        compiler_params=pltpu.CompilerParams(vmem_limit_bytes=60 * 1024 * 1024),
        name="pack",
    )(block_mask, signal, cotangent, filter_raw)
    received = lax.all_to_all(packed, everyone, split_axis=0, concat_axis=0, tiled=True)
    results = pl.pallas_call(
        functools.partial(spectral_kernel, blocks, rows, replicas, group, factor),
        out_shape=jax.ShapeDtypeStruct((count, group * (pair + half), LANES), jnp.bfloat16),
        in_specs=[VMEM] * 9,
        out_specs=VMEM,
        scratch_shapes=[
            pltpu.VMEM((count * group * own, LANES), jnp.float32),
            pltpu.VMEM((2 * blocks * group * half, LANES), jnp.float32),
        ],
        compiler_params=LIMIT,
        name="spectral",
    )(received, *tables)
    returned = lax.all_to_all(results, everyone, split_axis=0, concat_axis=0, tiled=True)
    own_taps = returned[:, group * pair :, :]
    other_taps = lax.ppermute(own_taps, "dp", [(i, i ^ 1) for i in range(replicas)])
    conv_out, signal_grad = pl.pallas_call(
        functools.partial(unpack_kernel, group),
        out_shape=[jax.ShapeDtypeStruct(signal.shape, jnp.bfloat16)] * 2,
        in_specs=[SMEM, VMEM],
        out_specs=[HBM, HBM],
        scratch_shapes=[
            pltpu.VMEM((count * group * pair, LANES), jnp.float32),
            pltpu.VMEM((tokens, channels), jnp.bfloat16),
            pltpu.VMEM((tokens, channels), jnp.bfloat16),
            pltpu.SemaphoreType.DMA((2 * rows,)),
        ],
        compiler_params=LIMIT,
        name="unpack",
    )(block_mask, returned)
    filter_grad = pl.pallas_call(
        functools.partial(unpack_taps_kernel, group),
        out_shape=jax.ShapeDtypeStruct(filter_raw.shape, jnp.bfloat16),
        in_specs=[VMEM, VMEM],
        out_specs=HBM,
        scratch_shapes=[
            pltpu.VMEM((2 * count * group * half, LANES), jnp.float32),
            pltpu.VMEM((tokens, channels), jnp.bfloat16),
            pltpu.SemaphoreType.DMA((2 * half,)),
        ],
        compiler_params=LIMIT,
        name="unpack_taps",
    )(own_taps, other_taps)
    return conv_out, signal_grad, filter_grad


def solution(mesh):
    placed = (P("dp", "seq", None), P("seq", None), P("dp", "seq", None), P("dp", "seq"))
    return jax.shard_map(
        per_device,
        mesh=mesh,
        in_specs=placed,
        out_specs=(P("dp", "seq", None), P("dp", "seq", None), P("seq", None)),
        check_vma=False,
    )
```

```python
import functools
import math

import jax
import jax.numpy as jnp
import ml_dtypes
import numpy as np
from jax import lax
from jax.experimental import pallas as pl
from jax.experimental.pallas import tpu as pltpu
from jax.sharding import PartitionSpec as P

LANES = 128
BLK = 1024
BF16 = ml_dtypes.bfloat16


def wave(product, period):
    angle = 2.0 * np.pi / period * (product % period)
    return np.cos(angle), np.sin(angle)


def make_tables(blocks, rows, replicas):
    coarse = blocks * rows
    freq = np.arange(coarse)
    lane = np.arange(LANES)
    own = rows // replicas
    half = rows // 2
    grid_j, grid_r = np.meshgrid(np.arange(blocks), np.arange(rows), indexing="ij")
    plain = grid_j * rows + grid_r
    cos_a, sin_a = wave((4 * freq[:, None] + 1) * np.arange(coarse)[None, :], 4 * coarse)
    first = np.zeros((2, 2, coarse, blocks, 2, rows))
    last = np.zeros((blocks, 2, rows, 2, 2, coarse))
    for which in range(2):
        first[which, 0, :, :, which, :] = cos_a[:, plain]
        first[which, 1, :, :, which, :] = -sin_a[:, plain]
        last[:, which, :, which, 0, :] = np.moveaxis(cos_a[:, plain], 0, 2)
        last[:, which, :, which, 1, :] = -np.moveaxis(sin_a[:, plain], 0, 2)
    taps = (
        np.arange(own)[:, None, None]
        + rows * np.arange(blocks)[None, :, None]
        + own * np.arange(replicas)[None, None, :]
    ).reshape(-1)
    first_taps = np.concatenate([cos_a[:, taps], -sin_a[:, taps]], axis=0)
    back = (
        np.arange(half)[:, None, None]
        + half * np.arange(2)[None, :, None]
        + rows * np.arange(blocks)[None, None, :]
    ).reshape(-1)
    last_taps = np.concatenate([cos_a[:, back], -sin_a[:, back]], axis=0).T
    twist_cos, twist_sin = wave((4 * freq[:, None] + 1) * lane[None, :], 4 * LANES * coarse)
    cos_l, sin_l = wave(lane[:, None] * lane[None, :], LANES)
    inner = np.block([[cos_l, -sin_l], [sin_l, cos_l]])
    inner_back = np.block([[cos_l, sin_l], [-sin_l, cos_l]])
    narrow = (
        first.reshape(4 * coarse, 2 * coarse),
        first_taps,
        inner,
        inner_back,
        last.reshape(2 * coarse, 4 * coarse),
        last_taps,
    )
    return tuple(t.astype(np.float32).astype(BF16) for t in narrow) + (
        twist_cos.astype(np.float32),
        twist_sin.astype(np.float32),
    )


def pack_kernel(
    own, group, count, mask_ref, signal_ref, grad_ref, filter_ref, send_ref,
    signal_buf, grad_buf, filter_buf, pair_scr, tap_scr, in_sems,
):
    tokens, channels = filter_ref.shape
    rows = tokens // LANES
    pair = 2 * rows
    block_rows = BLK // LANES
    parts = in_sems.shape[0] // 2
    part_rows = rows // parts
    start = pl.multiple_of(lax.axis_index("dp") * (own * LANES), own * LANES)
    filter_copy = pltpu.make_async_copy(
        filter_ref.at[pl.ds(start, own * LANES), :], filter_buf, in_sems.at[2 * parts]
    )
    copies = []
    for part in range(parts):
        span = pl.ds(part * part_rows * LANES, part_rows * LANES)
        copies.append(
            pltpu.make_async_copy(
                signal_ref.at[0, span, :], signal_buf.at[span, :], in_sems.at[2 * part]
            )
        )
        copies.append(
            pltpu.make_async_copy(
                grad_ref.at[0, span, :], grad_buf.at[span, :], in_sems.at[2 * part + 1]
            )
        )
    filter_copy.start()
    for copy in copies:
        copy.start()
    if group * count != channels:
        pair_scr[...] = jnp.zeros_like(pair_scr)
        tap_scr[...] = jnp.zeros_like(tap_scr)
    filter_copy.wait()
    for row in range(own):
        tap_scr[pl.ds(row, channels, stride=own), :] = (
            filter_buf[row * LANES : (row + 1) * LANES, :].astype(jnp.float32).T
        )
    for part in range(parts):
        places = range(part * part_rows, (part + 1) * part_rows)
        copies[2 * part].wait()
        for row in places:
            keep = mask_ref[0, row // block_rows].astype(jnp.float32)
            pair_scr[pl.ds(row, channels, stride=pair), :] = (
                signal_buf[row * LANES : (row + 1) * LANES, :].astype(jnp.float32).T * keep
            )
        copies[2 * part + 1].wait()
        for row in places:
            pair_scr[pl.ds(rows + row, channels, stride=pair), :] = (
                grad_buf[row * LANES : (row + 1) * LANES, :].astype(jnp.float32).T
            )
    for target in range(count):
        send_ref[target, : group * pair, :] = pair_scr[
            target * group * pair : (target + 1) * group * pair, :
        ].astype(jnp.bfloat16)
        send_ref[target, group * pair :, :] = tap_scr[
            target * group * own : (target + 1) * group * own, :
        ].astype(jnp.bfloat16)


def spectral_kernel(
    blocks, rows, replicas, group, factor,
    recv_ref, first_ref, first_taps_ref, inner_ref, inner_back_ref, last_ref, last_taps_ref,
    twist_cos_ref, twist_sin_ref, send_ref, tap_scr, back_scr,
):
    coarse = blocks * rows
    count = blocks * replicas
    pair = 2 * rows
    own = rows // replicas
    half = rows // 2
    tap_rows = group * own
    back_rows = group * half
    for source in range(count):
        tap_scr[source * tap_rows : (source + 1) * tap_rows, :] = recv_ref[
            source, group * pair :, :
        ].astype(jnp.float32)

    def dot(left, right):
        return jnp.dot(left, right, preferred_element_type=jnp.float32)

    def spread(index):
        offset = index * pair
        twist_cos = twist_cos_ref[...]
        twist_sin = twist_sin_ref[...]

        def turn(real, imag):
            return jnp.concatenate(
                [real * twist_cos + imag * twist_sin, imag * twist_cos - real * twist_sin], axis=1
            ).astype(jnp.bfloat16)

        taps = jnp.concatenate(
            [tap_scr[pl.ds(index * own + row, count, stride=tap_rows), :] for row in range(own)],
            axis=0,
        ).astype(jnp.bfloat16)
        wide_taps = dot(first_taps_ref[...], taps)
        data = jnp.concatenate(
            [
                jnp.concatenate(
                    [
                        recv_ref[block * replicas + seq, pl.ds(offset, pair), :]
                        for block in range(blocks)
                    ],
                    axis=0,
                )
                for seq in range(replicas)
            ],
            axis=1,
        )
        wide = dot(first_ref[...], data)
        turned = [turn(wide_taps[:coarse], wide_taps[coarse:])]
        for seq in range(replicas):
            part = wide[:, seq * LANES : (seq + 1) * LANES]
            for which in range(2):
                base = 2 * which * coarse
                turned.append(
                    turn(part[base : base + coarse], part[base + coarse : base + 2 * coarse])
                )
        return jnp.concatenate(turned, axis=0)

    def multiply(turned):
        spectrum = dot(turned, inner_ref[...])

        def pick(place):
            piece = spectrum[place * coarse : (place + 1) * coarse]
            return piece[:, :LANES], piece[:, LANES:]

        filter_real, filter_imag = pick(0)
        products = []
        weight_real = weight_imag = None
        for seq in range(replicas):
            signal_real, signal_imag = pick(1 + 2 * seq)
            grad_real, grad_imag = pick(2 + 2 * seq)
            out = (
                signal_real * filter_real - signal_imag * filter_imag,
                signal_real * filter_imag + signal_imag * filter_real,
            )
            into = (
                grad_real * filter_real + grad_imag * filter_imag,
                grad_imag * filter_real - grad_real * filter_imag,
            )
            term_real = grad_real * signal_real + grad_imag * signal_imag
            term_imag = grad_imag * signal_real - grad_real * signal_imag
            weight_real = term_real if weight_real is None else weight_real + term_real
            weight_imag = term_imag if weight_imag is None else weight_imag + term_imag
            products.append(jnp.concatenate(out, axis=1).astype(jnp.bfloat16))
            products.append(jnp.concatenate(into, axis=1).astype(jnp.bfloat16))
        products.append(
            jnp.concatenate([weight_real, weight_imag], axis=1).astype(jnp.bfloat16)
        )
        return jnp.concatenate(products, axis=0)

    def narrow(products):
        inverted = dot(products, inner_back_ref[...])
        twist_cos = twist_cos_ref[...]
        twist_sin = twist_sin_ref[...]

        def turn_back(place):
            piece = inverted[place * coarse : (place + 1) * coarse]
            real, imag = piece[:, :LANES], piece[:, LANES:]
            return jnp.concatenate(
                [real * twist_cos - imag * twist_sin, imag * twist_cos + real * twist_sin], axis=0
            ).astype(jnp.bfloat16)

        columns = jnp.concatenate(
            [
                jnp.concatenate([turn_back(2 * seq), turn_back(2 * seq + 1)], axis=0)
                for seq in range(replicas)
            ],
            axis=1,
        )
        return columns, turn_back(2 * replicas)

    def finish(index, columns, weight_column):
        offset = index * pair
        result = (dot(last_ref[...], columns) * factor).astype(jnp.bfloat16)
        for seq in range(replicas):
            for block in range(blocks):
                send_ref[block * replicas + seq, pl.ds(offset, pair), :] = result[
                    block * pair : (block + 1) * pair, seq * LANES : (seq + 1) * LANES
                ]
        weights = dot(last_taps_ref[...], weight_column) * factor
        for row in range(half):
            back_scr[pl.ds(index * half + row, 2 * blocks, stride=back_rows), :] = weights[
                row * 2 * blocks : (row + 1) * 2 * blocks
            ]

    turned, products, columns = {}, {}, {}
    for step in range(group + 3):
        if step >= 3:
            finish(step - 3, *columns.pop(step - 3))
        if 2 <= step < group + 2:
            columns[step - 2] = narrow(products.pop(step - 2))
        if 1 <= step < group + 1:
            products[step - 1] = multiply(turned.pop(step - 1))
        if step < group:
            turned[step] = spread(step)
    for target in range(count):
        place = target % replicas % 2 * blocks + target // replicas
        send_ref[target, group * pair :, :] = back_scr[
            place * back_rows : (place + 1) * back_rows, :
        ].astype(jnp.bfloat16)


def unpack_kernel(
    group, mask_ref, recv_ref, conv_ref, grad_ref, pair_scr, conv_buf, grad_buf, sems
):
    tokens, channels = conv_ref.shape[1:]
    rows = tokens // LANES
    pair = 2 * rows
    block_rows = BLK // LANES
    size = group * pair
    for source in range(recv_ref.shape[0]):
        pair_scr[source * size : (source + 1) * size, :] = recv_ref[source, :size, :].astype(
            jnp.float32
        )
    copies = []
    for row in range(rows):
        span = pl.ds(row * LANES, LANES)
        keep = mask_ref[0, row // block_rows].astype(jnp.float32)
        conv_buf[span, :] = pair_scr[pl.ds(row, channels, stride=pair), :].T.astype(jnp.bfloat16)
        copies.append(
            pltpu.make_async_copy(conv_buf.at[span, :], conv_ref.at[0, span, :], sems.at[2 * row])
        )
        copies[-1].start()
        grad_buf[span, :] = (
            pair_scr[pl.ds(rows + row, channels, stride=pair), :].T * keep
        ).astype(jnp.bfloat16)
        copies.append(
            pltpu.make_async_copy(
                grad_buf.at[span, :], grad_ref.at[0, span, :], sems.at[2 * row + 1]
            )
        )
        copies[-1].start()
    for copy in copies:
        copy.wait()


def unpack_taps_kernel(group, own_ref, other_ref, taps_ref, scr, taps_buf, sems):
    tokens, channels = taps_ref.shape
    half = tokens // LANES // 2
    size = group * half
    side = lax.rem(lax.axis_index("dp"), 2)
    copies = []
    for place, ref in enumerate((own_ref, other_ref)):
        base = place * ref.shape[0] * size
        for source in range(ref.shape[0]):
            scr[base + source * size : base + (source + 1) * size, :] = ref[source].astype(
                jnp.float32
            )
        start = jnp.where(side == place, 0, half * LANES)
        for row in range(half):
            slot = place * half + row
            span = pl.ds(slot * LANES, LANES)
            taps_buf[span, :] = scr[pl.ds(base + row, channels, stride=half), :].T.astype(
                jnp.bfloat16
            )
            goal = pl.ds(pl.multiple_of(start + row * LANES, LANES), LANES)
            copies.append(
                pltpu.make_async_copy(taps_buf.at[span, :], taps_ref.at[goal, :], sems.at[slot])
            )
            copies[-1].start()
    for copy in copies:
        copy.wait()


VMEM = pl.BlockSpec(memory_space=pltpu.VMEM)
SMEM = pl.BlockSpec(memory_space=pltpu.SMEM)
HBM = pl.BlockSpec(memory_space=pltpu.HBM)
LIMIT = pltpu.CompilerParams(vmem_limit_bytes=48 * 1024 * 1024)


def per_device(signal, filter_raw, cotangent, block_mask):
    tokens, channels = filter_raw.shape
    blocks = lax.axis_size("seq")
    replicas = lax.axis_size("dp")
    count = blocks * replicas
    group = -(-channels // count)
    rows = tokens // LANES
    pair = 2 * rows
    own = rows // replicas
    half = rows // 2
    total = tokens * blocks
    coarse = total // LANES
    factor = 1.0 / (total * math.sqrt(total))
    everyone = ("seq", "dp")
    tables = [jnp.asarray(t) for t in make_tables(blocks, rows, replicas)]

    inputs = (signal, cotangent, filter_raw)
    packed = pl.pallas_call(
        functools.partial(pack_kernel, own, group, count),
        out_shape=pltpu.VMEM((count, group * (pair + own), LANES), jnp.bfloat16),
        in_specs=[SMEM, HBM, HBM, HBM],
        out_specs=VMEM,
        scratch_shapes=[
            pltpu.VMEM((tokens, channels), jnp.bfloat16),
            pltpu.VMEM((tokens, channels), jnp.bfloat16),
            pltpu.VMEM((own * LANES, channels), jnp.bfloat16),
            pltpu.VMEM((count * group * pair, LANES), jnp.float32),
            pltpu.VMEM((count * group * own, LANES), jnp.float32),
            pltpu.SemaphoreType.DMA((5,)),
        ],
        compiler_params=LIMIT,
        name="pack",
    )(block_mask, *(pltpu.with_memory_space_constraint(x, pltpu.HBM) for x in inputs))
    received = lax.all_to_all(packed, everyone, split_axis=0, concat_axis=0, tiled=True)
    results = pl.pallas_call(
        functools.partial(spectral_kernel, blocks, rows, replicas, group, factor),
        out_shape=jax.ShapeDtypeStruct((count, group * (pair + half), LANES), jnp.bfloat16),
        in_specs=[VMEM] * 9,
        out_specs=VMEM,
        scratch_shapes=[
            pltpu.VMEM((count * group * own, LANES), jnp.float32),
            pltpu.VMEM((2 * blocks * group * half, LANES), jnp.float32),
        ],
        compiler_params=LIMIT,
        name="spectral",
    )(received, *tables)
    returned = lax.all_to_all(results, everyone, split_axis=0, concat_axis=0, tiled=True)
    own_taps = returned[:, group * pair :, :]
    other_taps = lax.ppermute(own_taps, "dp", [(i, i ^ 1) for i in range(replicas)])
    conv_out, signal_grad = pl.pallas_call(
        functools.partial(unpack_kernel, group),
        out_shape=[jax.ShapeDtypeStruct(signal.shape, jnp.bfloat16)] * 2,
        in_specs=[SMEM, VMEM],
        out_specs=[HBM, HBM],
        scratch_shapes=[
            pltpu.VMEM((count * group * pair, LANES), jnp.float32),
            pltpu.VMEM((tokens, channels), jnp.bfloat16),
            pltpu.VMEM((tokens, channels), jnp.bfloat16),
            pltpu.SemaphoreType.DMA((2 * rows,)),
        ],
        compiler_params=LIMIT,
        name="unpack",
    )(block_mask, returned)
    filter_grad = pl.pallas_call(
        functools.partial(unpack_taps_kernel, group),
        out_shape=jax.ShapeDtypeStruct(filter_raw.shape, jnp.bfloat16),
        in_specs=[VMEM, VMEM],
        out_specs=HBM,
        scratch_shapes=[
            pltpu.VMEM((2 * count * group * half, LANES), jnp.float32),
            pltpu.VMEM((tokens, channels), jnp.bfloat16),
            pltpu.SemaphoreType.DMA((2 * half,)),
        ],
        compiler_params=LIMIT,
        name="unpack_taps",
    )(own_taps, other_taps)
    return conv_out, signal_grad, filter_grad


def solution(mesh):
    placed = (P("dp", "seq", None), P("seq", None), P("dp", "seq", None), P("dp", "seq"))
    return jax.shard_map(
        per_device,
        mesh=mesh,
        in_specs=placed,
        out_specs=(P("dp", "seq", None), P("dp", "seq", None), P("seq", None)),
        check_vma=False,
    )
```

```python
import functools
import math

import jax
import jax.numpy as jnp
import ml_dtypes
import numpy as np
from jax import lax
from jax.experimental import pallas as pl
from jax.experimental.pallas import tpu as pltpu
from jax.sharding import PartitionSpec as P

LANES = 128
BLK = 1024
BF16 = ml_dtypes.bfloat16


def wave(product, period):
    angle = 2.0 * np.pi / period * (product % period)
    return np.cos(angle), np.sin(angle)


def make_tables(blocks, rows, replicas):
    coarse = blocks * rows
    freq = np.arange(coarse)
    lane = np.arange(LANES)
    own = rows // replicas
    half = rows // 2
    grid_j, grid_r = np.meshgrid(np.arange(blocks), np.arange(rows), indexing="ij")
    plain = grid_j * rows + grid_r
    cos_a, sin_a = wave((4 * freq[:, None] + 1) * np.arange(coarse)[None, :], 4 * coarse)
    first = np.zeros((2, 2, coarse, blocks, 2, rows))
    last = np.zeros((blocks, 2, rows, 2, 2, coarse))
    for which in range(2):
        first[which, 0, :, :, which, :] = cos_a[:, plain]
        first[which, 1, :, :, which, :] = -sin_a[:, plain]
        last[:, which, :, which, 0, :] = np.moveaxis(cos_a[:, plain], 0, 2)
        last[:, which, :, which, 1, :] = -np.moveaxis(sin_a[:, plain], 0, 2)
    taps = (
        np.arange(own)[:, None, None]
        + rows * np.arange(blocks)[None, :, None]
        + own * np.arange(replicas)[None, None, :]
    ).reshape(-1)
    first_taps = np.concatenate([cos_a[:, taps], -sin_a[:, taps]], axis=0)
    back = (
        np.arange(half)[:, None, None]
        + half * np.arange(2)[None, :, None]
        + rows * np.arange(blocks)[None, None, :]
    ).reshape(-1)
    last_taps = np.concatenate([cos_a[:, back], -sin_a[:, back]], axis=0).T
    twist_cos, twist_sin = wave((4 * freq[:, None] + 1) * lane[None, :], 4 * LANES * coarse)
    cos_l, sin_l = wave(lane[:, None] * lane[None, :], LANES)
    inner = np.block([[cos_l, -sin_l], [sin_l, cos_l]])
    inner_back = np.block([[cos_l, sin_l], [-sin_l, cos_l]])
    narrow = (
        first.reshape(4 * coarse, 2 * coarse),
        first_taps,
        inner,
        inner_back,
        last.reshape(2 * coarse, 4 * coarse),
        last_taps,
    )
    return tuple(t.astype(np.float32).astype(BF16) for t in narrow) + (
        twist_cos.astype(np.float32),
        twist_sin.astype(np.float32),
    )


def pack_kernel(
    own, group, count, mask_ref, signal_ref, grad_ref, filter_ref, send_ref,
    signal_buf, grad_buf, filter_buf, pair_scr, tap_scr, in_sems,
):
    tokens, channels = filter_ref.shape
    rows = tokens // LANES
    pair = 2 * rows
    block_rows = BLK // LANES
    parts = in_sems.shape[0] // 2
    part_rows = rows // parts
    start = pl.multiple_of(lax.axis_index("dp") * (own * LANES), own * LANES)
    filter_copy = pltpu.make_async_copy(
        filter_ref.at[pl.ds(start, own * LANES), :], filter_buf, in_sems.at[2 * parts]
    )
    copies = []
    for part in range(parts):
        span = pl.ds(part * part_rows * LANES, part_rows * LANES)
        copies.append(
            pltpu.make_async_copy(
                signal_ref.at[0, span, :], signal_buf.at[span, :], in_sems.at[2 * part]
            )
        )
        copies.append(
            pltpu.make_async_copy(
                grad_ref.at[0, span, :], grad_buf.at[span, :], in_sems.at[2 * part + 1]
            )
        )
    filter_copy.start()
    for copy in copies:
        copy.start()
    if group * count != channels:
        pair_scr[...] = jnp.zeros_like(pair_scr)
        tap_scr[...] = jnp.zeros_like(tap_scr)
    filter_copy.wait()
    for row in range(own):
        tap_scr[pl.ds(row, channels, stride=own), :] = (
            filter_buf[row * LANES : (row + 1) * LANES, :].astype(jnp.float32).T
        )
    for part in range(parts):
        places = range(part * part_rows, (part + 1) * part_rows)
        copies[2 * part].wait()
        for row in places:
            keep = mask_ref[0, row // block_rows].astype(jnp.float32)
            pair_scr[pl.ds(row, channels, stride=pair), :] = (
                signal_buf[row * LANES : (row + 1) * LANES, :].astype(jnp.float32).T * keep
            )
        copies[2 * part + 1].wait()
        for row in places:
            pair_scr[pl.ds(rows + row, channels, stride=pair), :] = (
                grad_buf[row * LANES : (row + 1) * LANES, :].astype(jnp.float32).T
            )
    for target in range(count):
        send_ref[target, : group * pair, :] = pair_scr[
            target * group * pair : (target + 1) * group * pair, :
        ].astype(jnp.bfloat16)
        send_ref[target, group * pair :, :] = tap_scr[
            target * group * own : (target + 1) * group * own, :
        ].astype(jnp.bfloat16)


def spectral_kernel(
    blocks, rows, replicas, group, factor,
    recv_ref, first_ref, first_taps_ref, inner_ref, inner_back_ref, last_ref, last_taps_ref,
    twist_cos_ref, twist_sin_ref, send_ref, tap_scr, back_scr,
):
    coarse = blocks * rows
    count = blocks * replicas
    pair = 2 * rows
    own = rows // replicas
    half = rows // 2
    tap_rows = group * own
    back_rows = group * half
    for source in range(count):
        tap_scr[source * tap_rows : (source + 1) * tap_rows, :] = recv_ref[
            source, group * pair :, :
        ].astype(jnp.float32)

    def dot(left, right):
        return jnp.dot(left, right, preferred_element_type=jnp.float32)

    def spread(index):
        offset = index * pair
        twist_cos = twist_cos_ref[...]
        twist_sin = twist_sin_ref[...]

        def turn(real, imag):
            return jnp.concatenate(
                [real * twist_cos + imag * twist_sin, imag * twist_cos - real * twist_sin], axis=1
            ).astype(jnp.bfloat16)

        taps = jnp.concatenate(
            [tap_scr[pl.ds(index * own + row, count, stride=tap_rows), :] for row in range(own)],
            axis=0,
        ).astype(jnp.bfloat16)
        wide_taps = dot(first_taps_ref[...], taps)
        data = jnp.concatenate(
            [
                jnp.concatenate(
                    [
                        recv_ref[block * replicas + seq, pl.ds(offset, pair), :]
                        for block in range(blocks)
                    ],
                    axis=0,
                )
                for seq in range(replicas)
            ],
            axis=1,
        )
        wide = dot(first_ref[...], data)
        turned = [turn(wide_taps[:coarse], wide_taps[coarse:])]
        for seq in range(replicas):
            part = wide[:, seq * LANES : (seq + 1) * LANES]
            for which in range(2):
                base = 2 * which * coarse
                turned.append(
                    turn(part[base : base + coarse], part[base + coarse : base + 2 * coarse])
                )
        return jnp.concatenate(turned, axis=0)

    def multiply(turned):
        spectrum = dot(turned, inner_ref[...])

        def pick(place):
            piece = spectrum[place * coarse : (place + 1) * coarse]
            return piece[:, :LANES], piece[:, LANES:]

        filter_real, filter_imag = pick(0)
        products = []
        weight_real = weight_imag = None
        for seq in range(replicas):
            signal_real, signal_imag = pick(1 + 2 * seq)
            grad_real, grad_imag = pick(2 + 2 * seq)
            out = (
                signal_real * filter_real - signal_imag * filter_imag,
                signal_real * filter_imag + signal_imag * filter_real,
            )
            into = (
                grad_real * filter_real + grad_imag * filter_imag,
                grad_imag * filter_real - grad_real * filter_imag,
            )
            term_real = grad_real * signal_real + grad_imag * signal_imag
            term_imag = grad_imag * signal_real - grad_real * signal_imag
            weight_real = term_real if weight_real is None else weight_real + term_real
            weight_imag = term_imag if weight_imag is None else weight_imag + term_imag
            products.append(jnp.concatenate(out, axis=1).astype(jnp.bfloat16))
            products.append(jnp.concatenate(into, axis=1).astype(jnp.bfloat16))
        products.append(
            jnp.concatenate([weight_real, weight_imag], axis=1).astype(jnp.bfloat16)
        )
        return jnp.concatenate(products, axis=0)

    def narrow(products):
        inverted = dot(products, inner_back_ref[...])
        twist_cos = twist_cos_ref[...]
        twist_sin = twist_sin_ref[...]

        def turn_back(place):
            piece = inverted[place * coarse : (place + 1) * coarse]
            real, imag = piece[:, :LANES], piece[:, LANES:]
            return jnp.concatenate(
                [real * twist_cos - imag * twist_sin, imag * twist_cos + real * twist_sin], axis=0
            ).astype(jnp.bfloat16)

        columns = jnp.concatenate(
            [
                jnp.concatenate([turn_back(2 * seq), turn_back(2 * seq + 1)], axis=0)
                for seq in range(replicas)
            ],
            axis=1,
        )
        return columns, turn_back(2 * replicas)

    def finish(index, columns, weight_column):
        offset = index * pair
        result = (dot(last_ref[...], columns) * factor).astype(jnp.bfloat16)
        for seq in range(replicas):
            for block in range(blocks):
                send_ref[block * replicas + seq, pl.ds(offset, pair), :] = result[
                    block * pair : (block + 1) * pair, seq * LANES : (seq + 1) * LANES
                ]
        weights = dot(last_taps_ref[...], weight_column) * factor
        for row in range(half):
            back_scr[pl.ds(index * half + row, 2 * blocks, stride=back_rows), :] = weights[
                row * 2 * blocks : (row + 1) * 2 * blocks
            ]

    turned, products, columns = {}, {}, {}
    for step in range(group + 3):
        if step >= 3:
            finish(step - 3, *columns.pop(step - 3))
        if 2 <= step < group + 2:
            columns[step - 2] = narrow(products.pop(step - 2))
        if 1 <= step < group + 1:
            products[step - 1] = multiply(turned.pop(step - 1))
        if step < group:
            turned[step] = spread(step)
    for target in range(count):
        place = target % replicas % 2 * blocks + target // replicas
        send_ref[target, group * pair :, :] = back_scr[
            place * back_rows : (place + 1) * back_rows, :
        ].astype(jnp.bfloat16)


def unpack_kernel(
    group, mask_ref, recv_ref, conv_ref, grad_ref, pair_scr, conv_buf, grad_buf, sems
):
    tokens, channels = conv_ref.shape[1:]
    rows = tokens // LANES
    pair = 2 * rows
    block_rows = BLK // LANES
    size = group * pair
    for source in range(recv_ref.shape[0]):
        pair_scr[source * size : (source + 1) * size, :] = recv_ref[source, :size, :].astype(
            jnp.float32
        )
    copies = []
    for row in range(rows):
        span = pl.ds(row * LANES, LANES)
        keep = mask_ref[0, row // block_rows].astype(jnp.float32)
        conv_buf[span, :] = pair_scr[pl.ds(row, channels, stride=pair), :].T.astype(jnp.bfloat16)
        copies.append(
            pltpu.make_async_copy(conv_buf.at[span, :], conv_ref.at[0, span, :], sems.at[2 * row])
        )
        copies[-1].start()
        grad_buf[span, :] = (
            pair_scr[pl.ds(rows + row, channels, stride=pair), :].T * keep
        ).astype(jnp.bfloat16)
        copies.append(
            pltpu.make_async_copy(
                grad_buf.at[span, :], grad_ref.at[0, span, :], sems.at[2 * row + 1]
            )
        )
        copies[-1].start()
    for copy in copies:
        copy.wait()


def unpack_taps_kernel(group, own_ref, other_ref, taps_ref, scr, taps_buf, sems):
    tokens, channels = taps_ref.shape
    half = tokens // LANES // 2
    size = group * half
    side = lax.rem(lax.axis_index("dp"), 2)
    copies = []
    for place, ref in enumerate((own_ref, other_ref)):
        base = place * ref.shape[0] * size
        for source in range(ref.shape[0]):
            scr[base + source * size : base + (source + 1) * size, :] = ref[source].astype(
                jnp.float32
            )
        start = jnp.where(side == place, 0, half * LANES)
        for row in range(half):
            slot = place * half + row
            span = pl.ds(slot * LANES, LANES)
            taps_buf[span, :] = scr[pl.ds(base + row, channels, stride=half), :].T.astype(
                jnp.bfloat16
            )
            goal = pl.ds(pl.multiple_of(start + row * LANES, LANES), LANES)
            copies.append(
                pltpu.make_async_copy(taps_buf.at[span, :], taps_ref.at[goal, :], sems.at[slot])
            )
            copies[-1].start()
    for copy in copies:
        copy.wait()


VMEM = pl.BlockSpec(memory_space=pltpu.VMEM)
SMEM = pl.BlockSpec(memory_space=pltpu.SMEM)
HBM = pl.BlockSpec(memory_space=pltpu.HBM)
LIMIT = pltpu.CompilerParams(vmem_limit_bytes=48 * 1024 * 1024)


def per_device(signal, filter_raw, cotangent, block_mask):
    tokens, channels = filter_raw.shape
    blocks = lax.axis_size("seq")
    replicas = lax.axis_size("dp")
    count = blocks * replicas
    group = -(-channels // count)
    rows = tokens // LANES
    pair = 2 * rows
    own = rows // replicas
    half = rows // 2
    total = tokens * blocks
    coarse = total // LANES
    factor = 1.0 / (total * math.sqrt(total))
    everyone = ("seq", "dp")
    tables = [jnp.asarray(t) for t in make_tables(blocks, rows, replicas)]

    inputs = (signal, cotangent, filter_raw)
    packed = pl.pallas_call(
        functools.partial(pack_kernel, own, group, count),
        out_shape=pltpu.VMEM((count, group * (pair + own), LANES), jnp.bfloat16),
        in_specs=[SMEM, HBM, HBM, HBM],
        out_specs=VMEM,
        scratch_shapes=[
            pltpu.VMEM((tokens, channels), jnp.bfloat16),
            pltpu.VMEM((tokens, channels), jnp.bfloat16),
            pltpu.VMEM((own * LANES, channels), jnp.bfloat16),
            pltpu.VMEM(((count * group + 1) * pair, LANES), jnp.float32),
            pltpu.VMEM(((count * group + 1) * own, LANES), jnp.float32),
            pltpu.SemaphoreType.DMA((5,)),
        ],
        compiler_params=LIMIT,
        name="pack",
    )(block_mask, *(pltpu.with_memory_space_constraint(x, pltpu.HBM) for x in inputs))
    received = lax.all_to_all(packed, everyone, split_axis=0, concat_axis=0, tiled=True)
    results = pl.pallas_call(
        functools.partial(spectral_kernel, blocks, rows, replicas, group, factor),
        out_shape=jax.ShapeDtypeStruct((count, group * (pair + half), LANES), jnp.bfloat16),
        in_specs=[VMEM] * 9,
        out_specs=VMEM,
        scratch_shapes=[
            pltpu.VMEM(((count + 1) * group * own, LANES), jnp.float32),
            pltpu.VMEM(((2 * blocks + 1) * group * half, LANES), jnp.float32),
        ],
        compiler_params=LIMIT,
        name="spectral",
    )(received, *tables)
    returned = lax.all_to_all(results, everyone, split_axis=0, concat_axis=0, tiled=True)
    own_taps = returned[:, group * pair :, :]
    other_taps = lax.ppermute(own_taps, "dp", [(i, i ^ 1) for i in range(replicas)])
    conv_out, signal_grad = pl.pallas_call(
        functools.partial(unpack_kernel, group),
        out_shape=[jax.ShapeDtypeStruct(signal.shape, jnp.bfloat16)] * 2,
        in_specs=[SMEM, VMEM],
        out_specs=[HBM, HBM],
        scratch_shapes=[
            pltpu.VMEM(((count * group + 1) * pair, LANES), jnp.float32),
            pltpu.VMEM((tokens, channels), jnp.bfloat16),
            pltpu.VMEM((tokens, channels), jnp.bfloat16),
            pltpu.SemaphoreType.DMA((2 * rows,)),
        ],
        compiler_params=LIMIT,
        name="unpack",
    )(block_mask, returned)
    filter_grad = pl.pallas_call(
        functools.partial(unpack_taps_kernel, group),
        out_shape=jax.ShapeDtypeStruct(filter_raw.shape, jnp.bfloat16),
        in_specs=[VMEM, VMEM],
        out_specs=HBM,
        scratch_shapes=[
            pltpu.VMEM(((2 * count * group + 1) * half, LANES), jnp.float32),
            pltpu.VMEM((tokens, channels), jnp.bfloat16),
            pltpu.SemaphoreType.DMA((2 * half,)),
        ],
        compiler_params=LIMIT,
        name="unpack_taps",
    )(own_taps, other_taps)
    return conv_out, signal_grad, filter_grad


def solution(mesh):
    placed = (P("dp", "seq", None), P("seq", None), P("dp", "seq", None), P("dp", "seq"))
    return jax.shard_map(
        per_device,
        mesh=mesh,
        in_specs=placed,
        out_specs=(P("dp", "seq", None), P("dp", "seq", None), P("seq", None)),
        check_vma=False,
    )
```

```python
import functools
import math

import jax
import jax.numpy as jnp
import ml_dtypes
import numpy as np
from jax import lax
from jax.experimental import pallas as pl
from jax.experimental.pallas import tpu as pltpu
from jax.sharding import PartitionSpec as P

LANES = 128
BLK = 1024
PAD = 1
BF16 = ml_dtypes.bfloat16


def wave(product, period):
    angle = 2.0 * np.pi / period * (product % period)
    return np.cos(angle), np.sin(angle)


def make_tables(blocks, rows, replicas):
    coarse = blocks * rows
    freq = np.arange(coarse)
    lane = np.arange(LANES)
    own = rows // replicas
    half = rows // 2
    grid_j, grid_r = np.meshgrid(np.arange(blocks), np.arange(rows), indexing="ij")
    plain = grid_j * rows + grid_r
    cos_a, sin_a = wave((4 * freq[:, None] + 1) * np.arange(coarse)[None, :], 4 * coarse)
    first = np.zeros((2, 2, coarse, blocks, 2, rows))
    last = np.zeros((blocks, 2, rows, 2, 2, coarse))
    for which in range(2):
        first[which, 0, :, :, which, :] = cos_a[:, plain]
        first[which, 1, :, :, which, :] = -sin_a[:, plain]
        last[:, which, :, which, 0, :] = np.moveaxis(cos_a[:, plain], 0, 2)
        last[:, which, :, which, 1, :] = -np.moveaxis(sin_a[:, plain], 0, 2)
    taps = (
        np.arange(own)[:, None, None]
        + rows * np.arange(blocks)[None, :, None]
        + own * np.arange(replicas)[None, None, :]
    ).reshape(-1)
    first_taps = np.concatenate([cos_a[:, taps], -sin_a[:, taps]], axis=0)
    back = (
        np.arange(half)[:, None, None]
        + half * np.arange(2)[None, :, None]
        + rows * np.arange(blocks)[None, None, :]
    ).reshape(-1)
    last_taps = np.concatenate([cos_a[:, back], -sin_a[:, back]], axis=0).T
    twist_cos, twist_sin = wave((4 * freq[:, None] + 1) * lane[None, :], 4 * LANES * coarse)
    cos_l, sin_l = wave(lane[:, None] * lane[None, :], LANES)
    inner = np.block([[cos_l, -sin_l], [sin_l, cos_l]])
    inner_back = np.block([[cos_l, sin_l], [-sin_l, cos_l]])
    narrow = (
        first.reshape(4 * coarse, 2 * coarse),
        first_taps,
        inner,
        inner_back,
        last.reshape(2 * coarse, 4 * coarse),
        last_taps,
    )
    return tuple(t.astype(np.float32).astype(BF16) for t in narrow) + (
        twist_cos.astype(np.float32),
        twist_sin.astype(np.float32),
    )


def pack_kernel(
    own, group, count, mask_ref, signal_ref, grad_ref, filter_ref, send_ref,
    signal_buf, grad_buf, filter_buf, pair_scr, tap_scr, in_sems,
):
    tokens, channels = filter_ref.shape
    rows = tokens // LANES
    pair = 2 * rows
    pitch = pair + PAD
    block_rows = BLK // LANES
    parts = in_sems.shape[0] // 2
    part_rows = rows // parts
    start = pl.multiple_of(lax.axis_index("dp") * (own * LANES), own * LANES)
    filter_copy = pltpu.make_async_copy(
        filter_ref.at[pl.ds(start, own * LANES), :], filter_buf, in_sems.at[2 * parts]
    )
    copies = []
    for part in range(parts):
        span = pl.ds(part * part_rows * LANES, part_rows * LANES)
        copies.append(
            pltpu.make_async_copy(
                signal_ref.at[0, span, :], signal_buf.at[span, :], in_sems.at[2 * part]
            )
        )
        copies.append(
            pltpu.make_async_copy(
                grad_ref.at[0, span, :], grad_buf.at[span, :], in_sems.at[2 * part + 1]
            )
        )
    filter_copy.start()
    for copy in copies:
        copy.start()
    if group * count != channels:
        pair_scr[...] = jnp.zeros_like(pair_scr)
        tap_scr[...] = jnp.zeros_like(tap_scr)
    filter_copy.wait()
    for row in range(own):
        tap_scr[pl.ds(row, channels, stride=own), :] = (
            filter_buf[row * LANES : (row + 1) * LANES, :].astype(jnp.float32).T
        )
    for part in range(parts):
        places = range(part * part_rows, (part + 1) * part_rows)
        copies[2 * part].wait()
        for row in places:
            keep = mask_ref[0, row // block_rows].astype(jnp.float32)
            pair_scr[pl.ds(row, channels, stride=pitch), :] = (
                signal_buf[row * LANES : (row + 1) * LANES, :].astype(jnp.float32).T * keep
            )
        copies[2 * part + 1].wait()
        for row in places:
            pair_scr[pl.ds(rows + row, channels, stride=pitch), :] = (
                grad_buf[row * LANES : (row + 1) * LANES, :].astype(jnp.float32).T
            )
    for target in range(count):
        send_ref[target, : group * pair, :] = jnp.concatenate(
            [
                pair_scr[index * pitch : index * pitch + pair, :]
                for index in range(target * group, (target + 1) * group)
            ],
            axis=0,
        ).astype(jnp.bfloat16)
        send_ref[target, group * pair :, :] = tap_scr[
            target * group * own : (target + 1) * group * own, :
        ].astype(jnp.bfloat16)


def spectral_kernel(
    blocks, rows, replicas, group, factor,
    recv_ref, first_ref, first_taps_ref, inner_ref, inner_back_ref, last_ref, last_taps_ref,
    twist_cos_ref, twist_sin_ref, send_ref, tap_scr, back_scr,
):
    coarse = blocks * rows
    count = blocks * replicas
    pair = 2 * rows
    own = rows // replicas
    half = rows // 2
    tap_rows = group * own + PAD
    back_rows = group * half + PAD
    for source in range(count):
        tap_scr[source * tap_rows : source * tap_rows + group * own, :] = recv_ref[
            source, group * pair :, :
        ].astype(jnp.float32)

    def dot(left, right):
        return jnp.dot(left, right, preferred_element_type=jnp.float32)

    def spread(index):
        offset = index * pair
        twist_cos = twist_cos_ref[...]
        twist_sin = twist_sin_ref[...]

        def turn(real, imag):
            return jnp.concatenate(
                [real * twist_cos + imag * twist_sin, imag * twist_cos - real * twist_sin], axis=1
            ).astype(jnp.bfloat16)

        taps = jnp.concatenate(
            [tap_scr[pl.ds(index * own + row, count, stride=tap_rows), :] for row in range(own)],
            axis=0,
        ).astype(jnp.bfloat16)
        wide_taps = dot(first_taps_ref[...], taps)
        data = jnp.concatenate(
            [
                jnp.concatenate(
                    [
                        recv_ref[block * replicas + seq, pl.ds(offset, pair), :]
                        for block in range(blocks)
                    ],
                    axis=0,
                )
                for seq in range(replicas)
            ],
            axis=1,
        )
        wide = dot(first_ref[...], data)
        turned = [turn(wide_taps[:coarse], wide_taps[coarse:])]
        for seq in range(replicas):
            part = wide[:, seq * LANES : (seq + 1) * LANES]
            for which in range(2):
                base = 2 * which * coarse
                turned.append(
                    turn(part[base : base + coarse], part[base + coarse : base + 2 * coarse])
                )
        return jnp.concatenate(turned, axis=0)

    def multiply(turned):
        spectrum = dot(turned, inner_ref[...])

        def pick(place):
            piece = spectrum[place * coarse : (place + 1) * coarse]
            return piece[:, :LANES], piece[:, LANES:]

        filter_real, filter_imag = pick(0)
        products = []
        weight_real = weight_imag = None
        for seq in range(replicas):
            signal_real, signal_imag = pick(1 + 2 * seq)
            grad_real, grad_imag = pick(2 + 2 * seq)
            out = (
                signal_real * filter_real - signal_imag * filter_imag,
                signal_real * filter_imag + signal_imag * filter_real,
            )
            into = (
                grad_real * filter_real + grad_imag * filter_imag,
                grad_imag * filter_real - grad_real * filter_imag,
            )
            term_real = grad_real * signal_real + grad_imag * signal_imag
            term_imag = grad_imag * signal_real - grad_real * signal_imag
            weight_real = term_real if weight_real is None else weight_real + term_real
            weight_imag = term_imag if weight_imag is None else weight_imag + term_imag
            products.append(jnp.concatenate(out, axis=1).astype(jnp.bfloat16))
            products.append(jnp.concatenate(into, axis=1).astype(jnp.bfloat16))
        products.append(
            jnp.concatenate([weight_real, weight_imag], axis=1).astype(jnp.bfloat16)
        )
        return jnp.concatenate(products, axis=0)

    def narrow(products):
        inverted = dot(products, inner_back_ref[...])
        twist_cos = twist_cos_ref[...]
        twist_sin = twist_sin_ref[...]

        def turn_back(place):
            piece = inverted[place * coarse : (place + 1) * coarse]
            real, imag = piece[:, :LANES], piece[:, LANES:]
            return jnp.concatenate(
                [real * twist_cos - imag * twist_sin, imag * twist_cos + real * twist_sin], axis=0
            ).astype(jnp.bfloat16)

        columns = jnp.concatenate(
            [
                jnp.concatenate([turn_back(2 * seq), turn_back(2 * seq + 1)], axis=0)
                for seq in range(replicas)
            ],
            axis=1,
        )
        return columns, turn_back(2 * replicas)

    def finish(index, columns, weight_column):
        offset = index * pair
        result = (dot(last_ref[...], columns) * factor).astype(jnp.bfloat16)
        for seq in range(replicas):
            for block in range(blocks):
                send_ref[block * replicas + seq, pl.ds(offset, pair), :] = result[
                    block * pair : (block + 1) * pair, seq * LANES : (seq + 1) * LANES
                ]
        weights = dot(last_taps_ref[...], weight_column) * factor
        for row in range(half):
            back_scr[pl.ds(index * half + row, 2 * blocks, stride=back_rows), :] = weights[
                row * 2 * blocks : (row + 1) * 2 * blocks
            ]

    turned, products, columns = {}, {}, {}
    for step in range(group + 3):
        if step >= 3:
            finish(step - 3, *columns.pop(step - 3))
        if 2 <= step < group + 2:
            columns[step - 2] = narrow(products.pop(step - 2))
        if 1 <= step < group + 1:
            products[step - 1] = multiply(turned.pop(step - 1))
        if step < group:
            turned[step] = spread(step)
    for target in range(count):
        place = target % replicas % 2 * blocks + target // replicas
        send_ref[target, group * pair :, :] = back_scr[
            place * back_rows : place * back_rows + group * half, :
        ].astype(jnp.bfloat16)


def unpack_kernel(
    group, mask_ref, recv_ref, conv_ref, grad_ref, pair_scr, conv_buf, grad_buf, sems
):
    tokens, channels = conv_ref.shape[1:]
    rows = tokens // LANES
    pair = 2 * rows
    pitch = pair + PAD
    block_rows = BLK // LANES
    size = group * pair
    for source in range(recv_ref.shape[0]):
        whole = recv_ref[source, :size, :].astype(jnp.float32)
        for index in range(group):
            start = (source * group + index) * pitch
            pair_scr[start : start + pair, :] = whole[index * pair : (index + 1) * pair]
    copies = []
    for row in range(rows):
        span = pl.ds(row * LANES, LANES)
        keep = mask_ref[0, row // block_rows].astype(jnp.float32)
        conv_buf[span, :] = pair_scr[pl.ds(row, channels, stride=pitch), :].T.astype(jnp.bfloat16)
        copies.append(
            pltpu.make_async_copy(conv_buf.at[span, :], conv_ref.at[0, span, :], sems.at[2 * row])
        )
        copies[-1].start()
        grad_buf[span, :] = (
            pair_scr[pl.ds(rows + row, channels, stride=pitch), :].T * keep
        ).astype(jnp.bfloat16)
        copies.append(
            pltpu.make_async_copy(
                grad_buf.at[span, :], grad_ref.at[0, span, :], sems.at[2 * row + 1]
            )
        )
        copies[-1].start()
    for copy in copies:
        copy.wait()


def unpack_taps_kernel(group, own_ref, other_ref, taps_ref, scr, taps_buf, sems):
    tokens, channels = taps_ref.shape
    half = tokens // LANES // 2
    size = group * half
    side = lax.rem(lax.axis_index("dp"), 2)
    copies = []
    for place, ref in enumerate((own_ref, other_ref)):
        base = place * ref.shape[0] * size
        for source in range(ref.shape[0]):
            scr[base + source * size : base + (source + 1) * size, :] = ref[source].astype(
                jnp.float32
            )
        start = jnp.where(side == place, 0, half * LANES)
        for row in range(half):
            slot = place * half + row
            span = pl.ds(slot * LANES, LANES)
            taps_buf[span, :] = scr[pl.ds(base + row, channels, stride=half), :].T.astype(
                jnp.bfloat16
            )
            goal = pl.ds(pl.multiple_of(start + row * LANES, LANES), LANES)
            copies.append(
                pltpu.make_async_copy(taps_buf.at[span, :], taps_ref.at[goal, :], sems.at[slot])
            )
            copies[-1].start()
    for copy in copies:
        copy.wait()


VMEM = pl.BlockSpec(memory_space=pltpu.VMEM)
SMEM = pl.BlockSpec(memory_space=pltpu.SMEM)
HBM = pl.BlockSpec(memory_space=pltpu.HBM)
LIMIT = pltpu.CompilerParams(vmem_limit_bytes=48 * 1024 * 1024)


def per_device(signal, filter_raw, cotangent, block_mask):
    tokens, channels = filter_raw.shape
    blocks = lax.axis_size("seq")
    replicas = lax.axis_size("dp")
    count = blocks * replicas
    group = -(-channels // count)
    rows = tokens // LANES
    pair = 2 * rows
    own = rows // replicas
    half = rows // 2
    total = tokens * blocks
    coarse = total // LANES
    factor = 1.0 / (total * math.sqrt(total))
    everyone = ("seq", "dp")
    tables = [jnp.asarray(t) for t in make_tables(blocks, rows, replicas)]

    inputs = (signal, cotangent, filter_raw)
    packed = pl.pallas_call(
        functools.partial(pack_kernel, own, group, count),
        out_shape=pltpu.VMEM((count, group * (pair + own), LANES), jnp.bfloat16),
        in_specs=[SMEM, HBM, HBM, HBM],
        out_specs=VMEM,
        scratch_shapes=[
            pltpu.VMEM((tokens, channels), jnp.bfloat16),
            pltpu.VMEM((tokens, channels), jnp.bfloat16),
            pltpu.VMEM((own * LANES, channels), jnp.bfloat16),
            pltpu.VMEM(((count * group + 1) * (pair + PAD), LANES), jnp.float32),
            pltpu.VMEM(((count * group + 1) * own, LANES), jnp.float32),
            pltpu.SemaphoreType.DMA((5,)),
        ],
        compiler_params=LIMIT,
        name="pack",
    )(block_mask, *(pltpu.with_memory_space_constraint(x, pltpu.HBM) for x in inputs))
    received = lax.all_to_all(packed, everyone, split_axis=0, concat_axis=0, tiled=True)
    results = pl.pallas_call(
        functools.partial(spectral_kernel, blocks, rows, replicas, group, factor),
        out_shape=jax.ShapeDtypeStruct((count, group * (pair + half), LANES), jnp.bfloat16),
        in_specs=[VMEM] * 9,
        out_specs=VMEM,
        scratch_shapes=[
            pltpu.VMEM(((count + 1) * (group * own + PAD), LANES), jnp.float32),
            pltpu.VMEM(((2 * blocks + 1) * (group * half + PAD), LANES), jnp.float32),
        ],
        compiler_params=LIMIT,
        name="spectral",
    )(received, *tables)
    returned = lax.all_to_all(results, everyone, split_axis=0, concat_axis=0, tiled=True)
    own_taps = returned[:, group * pair :, :]
    other_taps = lax.ppermute(own_taps, "dp", [(i, i ^ 1) for i in range(replicas)])
    conv_out, signal_grad = pl.pallas_call(
        functools.partial(unpack_kernel, group),
        out_shape=[jax.ShapeDtypeStruct(signal.shape, jnp.bfloat16)] * 2,
        in_specs=[SMEM, VMEM],
        out_specs=[HBM, HBM],
        scratch_shapes=[
            pltpu.VMEM(((count * group + 1) * (pair + PAD), LANES), jnp.float32),
            pltpu.VMEM((tokens, channels), jnp.bfloat16),
            pltpu.VMEM((tokens, channels), jnp.bfloat16),
            pltpu.SemaphoreType.DMA((2 * rows,)),
        ],
        compiler_params=LIMIT,
        name="unpack",
    )(block_mask, returned)
    filter_grad = pl.pallas_call(
        functools.partial(unpack_taps_kernel, group),
        out_shape=jax.ShapeDtypeStruct(filter_raw.shape, jnp.bfloat16),
        in_specs=[VMEM, VMEM],
        out_specs=HBM,
        scratch_shapes=[
            pltpu.VMEM(((2 * count * group + 1) * half, LANES), jnp.float32),
            pltpu.VMEM((tokens, channels), jnp.bfloat16),
            pltpu.SemaphoreType.DMA((2 * half,)),
        ],
        compiler_params=LIMIT,
        name="unpack_taps",
    )(own_taps, other_taps)
    return conv_out, signal_grad, filter_grad


def solution(mesh):
    placed = (P("dp", "seq", None), P("seq", None), P("dp", "seq", None), P("dp", "seq"))
    return jax.shard_map(
        per_device,
        mesh=mesh,
        in_specs=placed,
        out_specs=(P("dp", "seq", None), P("dp", "seq", None), P("seq", None)),
        check_vma=False,
    )
```

```python
import functools
import math

import jax
import jax.numpy as jnp
import ml_dtypes
import numpy as np
from jax import lax
from jax.experimental import pallas as pl
from jax.experimental.pallas import tpu as pltpu
from jax.sharding import PartitionSpec as P

LANES = 128
BLK = 1024
PAD = 1
BF16 = ml_dtypes.bfloat16


def wave(product, period):
    angle = 2.0 * np.pi / period * (product % period)
    return np.cos(angle), np.sin(angle)


def slot_order(blocks, replicas):
    turns = [0] + list(range((blocks - 1) // 2, 0, -1))
    return [
        (2 * turn + odd, seq) for odd in range(2) for seq in range(replicas) for turn in turns
    ]


def make_tables(blocks, rows, replicas):
    coarse = blocks * rows
    freq = np.arange(coarse)
    lane = np.arange(LANES)
    own = rows // replicas
    half = rows // 2
    grid_j, grid_r = np.meshgrid(np.arange(blocks), np.arange(rows), indexing="ij")
    plain = grid_j * rows + grid_r
    cos_a, sin_a = wave((4 * freq[:, None] + 1) * np.arange(coarse)[None, :], 4 * coarse)
    first = np.zeros((2, 2, coarse, blocks, 2, rows))
    last = np.zeros((blocks, 2, rows, 2, 2, coarse))
    for which in range(2):
        first[which, 0, :, :, which, :] = cos_a[:, plain]
        first[which, 1, :, :, which, :] = -sin_a[:, plain]
        last[:, which, :, which, 0, :] = np.moveaxis(cos_a[:, plain], 0, 2)
        last[:, which, :, which, 1, :] = -np.moveaxis(sin_a[:, plain], 0, 2)
    starts = np.array([rows * block + own * seq for block, seq in slot_order(blocks, replicas)])
    taps = (np.arange(own)[:, None] + starts[None, :]).reshape(-1)
    first_taps = np.concatenate([cos_a[:, taps], -sin_a[:, taps]], axis=0)
    back = (
        np.arange(half)[:, None, None]
        + half * np.arange(2)[None, :, None]
        + rows * np.arange(blocks)[None, None, :]
    ).reshape(-1)
    last_taps = np.concatenate([cos_a[:, back], -sin_a[:, back]], axis=0).T
    twist_cos, twist_sin = wave((4 * freq[:, None] + 1) * lane[None, :], 4 * LANES * coarse)
    cos_l, sin_l = wave(lane[:, None] * lane[None, :], LANES)
    inner = np.block([[cos_l, -sin_l], [sin_l, cos_l]])
    inner_back = np.block([[cos_l, sin_l], [-sin_l, cos_l]])
    narrow = (
        first.reshape(4 * coarse, 2 * coarse),
        first_taps,
        inner,
        inner_back,
        last.reshape(2 * coarse, 4 * coarse),
        last_taps,
    )
    return tuple(t.astype(np.float32).astype(BF16) for t in narrow) + (
        twist_cos.astype(np.float32),
        twist_sin.astype(np.float32),
    )


def pack_kernel(
    own, group, count, mask_ref, signal_ref, grad_ref, filter_ref, send_ref,
    signal_buf, grad_buf, filter_buf, pair_scr, tap_scr, in_sems,
):
    tokens, channels = filter_ref.shape
    rows = tokens // LANES
    pair = 2 * rows
    pitch = pair + PAD
    block_rows = BLK // LANES
    parts = in_sems.shape[0] // 2
    part_rows = rows // parts
    start = pl.multiple_of(lax.axis_index("dp") * (own * LANES), own * LANES)
    filter_copy = pltpu.make_async_copy(
        filter_ref.at[pl.ds(start, own * LANES), :], filter_buf, in_sems.at[2 * parts]
    )
    copies = []
    for part in range(parts):
        span = pl.ds(part * part_rows * LANES, part_rows * LANES)
        copies.append(
            pltpu.make_async_copy(
                signal_ref.at[0, span, :], signal_buf.at[span, :], in_sems.at[2 * part]
            )
        )
        copies.append(
            pltpu.make_async_copy(
                grad_ref.at[0, span, :], grad_buf.at[span, :], in_sems.at[2 * part + 1]
            )
        )
    for copy in copies:
        copy.start()
    filter_copy.start()
    if group * count != channels:
        pair_scr[...] = jnp.zeros_like(pair_scr)
        tap_scr[...] = jnp.zeros_like(tap_scr)
    copies[0].wait()
    for row in range(rows):
        keep = mask_ref[0, row // block_rows].astype(jnp.float32)
        pair_scr[pl.ds(row, channels, stride=pitch), :] = (
            signal_buf[row * LANES : (row + 1) * LANES, :].astype(jnp.float32).T * keep
        )
    copies[1].wait()
    filter_copy.wait()
    for row in range(rows):
        pair_scr[pl.ds(rows + row, channels, stride=pitch), :] = (
            grad_buf[row * LANES : (row + 1) * LANES, :].astype(jnp.float32).T
        )
    for row in range(own):
        tap_scr[pl.ds(row, channels, stride=own), :] = (
            filter_buf[row * LANES : (row + 1) * LANES, :].astype(jnp.float32).T
        )
    for target in range(count):
        send_ref[target, : group * pair, :] = jnp.concatenate(
            [
                pair_scr[index * pitch : index * pitch + pair, :]
                for index in range(target * group, (target + 1) * group)
            ],
            axis=0,
        ).astype(jnp.bfloat16)
        send_ref[target, group * pair :, :] = tap_scr[
            target * group * own : (target + 1) * group * own, :
        ].astype(jnp.bfloat16)


def spectral_kernel(
    blocks, rows, replicas, group, factor,
    recv_ref, first_ref, first_taps_ref, inner_ref, inner_back_ref, last_ref, last_taps_ref,
    twist_cos_ref, twist_sin_ref, send_ref, tap_scr, back_scr,
):
    coarse = blocks * rows
    count = blocks * replicas
    pair = 2 * rows
    own = rows // replicas
    half = rows // 2
    slots = {place: slot for slot, place in enumerate(slot_order(blocks, replicas))}
    tap_rows = group * own + PAD
    back_rows = group * half + PAD
    for source in range(count):
        tap_scr[source * tap_rows : source * tap_rows + group * own, :] = recv_ref[
            source, group * pair :, :
        ].astype(jnp.float32)

    def dot(left, right):
        return jnp.dot(left, right, preferred_element_type=jnp.float32)

    def spread(index):
        offset = index * pair
        twist_cos = twist_cos_ref[...]
        twist_sin = twist_sin_ref[...]

        def turn(real, imag):
            return jnp.concatenate(
                [real * twist_cos + imag * twist_sin, imag * twist_cos - real * twist_sin], axis=1
            ).astype(jnp.bfloat16)

        taps = jnp.concatenate(
            [tap_scr[pl.ds(index * own + row, count, stride=tap_rows), :] for row in range(own)],
            axis=0,
        ).astype(jnp.bfloat16)
        wide_taps = dot(first_taps_ref[...], taps)
        data = jnp.concatenate(
            [
                jnp.concatenate(
                    [
                        recv_ref[slots[block, seq], pl.ds(offset, pair), :]
                        for block in range(blocks)
                    ],
                    axis=0,
                )
                for seq in range(replicas)
            ],
            axis=1,
        )
        wide = dot(first_ref[...], data)
        turned = [turn(wide_taps[:coarse], wide_taps[coarse:])]
        for seq in range(replicas):
            part = wide[:, seq * LANES : (seq + 1) * LANES]
            for which in range(2):
                base = 2 * which * coarse
                turned.append(
                    turn(part[base : base + coarse], part[base + coarse : base + 2 * coarse])
                )
        return jnp.concatenate(turned, axis=0)

    def multiply(turned):
        spectrum = dot(turned, inner_ref[...])

        def pick(place):
            piece = spectrum[place * coarse : (place + 1) * coarse]
            return piece[:, :LANES], piece[:, LANES:]

        filter_real, filter_imag = pick(0)
        products = []
        weight_real = weight_imag = None
        for seq in range(replicas):
            signal_real, signal_imag = pick(1 + 2 * seq)
            grad_real, grad_imag = pick(2 + 2 * seq)
            out = (
                signal_real * filter_real - signal_imag * filter_imag,
                signal_real * filter_imag + signal_imag * filter_real,
            )
            into = (
                grad_real * filter_real + grad_imag * filter_imag,
                grad_imag * filter_real - grad_real * filter_imag,
            )
            term_real = grad_real * signal_real + grad_imag * signal_imag
            term_imag = grad_imag * signal_real - grad_real * signal_imag
            weight_real = term_real if weight_real is None else weight_real + term_real
            weight_imag = term_imag if weight_imag is None else weight_imag + term_imag
            products.append(jnp.concatenate(out, axis=1).astype(jnp.bfloat16))
            products.append(jnp.concatenate(into, axis=1).astype(jnp.bfloat16))
        products.append(
            jnp.concatenate([weight_real, weight_imag], axis=1).astype(jnp.bfloat16)
        )
        return jnp.concatenate(products, axis=0)

    def narrow(products):
        inverted = dot(products, inner_back_ref[...])
        twist_cos = twist_cos_ref[...]
        twist_sin = twist_sin_ref[...]

        def turn_back(place):
            piece = inverted[place * coarse : (place + 1) * coarse]
            real, imag = piece[:, :LANES], piece[:, LANES:]
            return jnp.concatenate(
                [real * twist_cos - imag * twist_sin, imag * twist_cos + real * twist_sin], axis=0
            ).astype(jnp.bfloat16)

        columns = jnp.concatenate(
            [
                jnp.concatenate([turn_back(2 * seq), turn_back(2 * seq + 1)], axis=0)
                for seq in range(replicas)
            ],
            axis=1,
        )
        return columns, turn_back(2 * replicas)

    def finish(index, columns, weight_column):
        offset = index * pair
        result = (dot(last_ref[...], columns) * factor).astype(jnp.bfloat16)
        for seq in range(replicas):
            for block in range(blocks):
                send_ref[slots[block, seq], pl.ds(offset, pair), :] = result[
                    block * pair : (block + 1) * pair, seq * LANES : (seq + 1) * LANES
                ]
        weights = dot(last_taps_ref[...], weight_column) * factor
        for row in range(half):
            back_scr[pl.ds(index * half + row, 2 * blocks, stride=back_rows), :] = weights[
                row * 2 * blocks : (row + 1) * 2 * blocks
            ]

    turned, products, columns = {}, {}, {}
    for step in range(group + 3):
        if step >= 3:
            finish(step - 3, *columns.pop(step - 3))
        if 2 <= step < group + 2:
            columns[step - 2] = narrow(products.pop(step - 2))
        if 1 <= step < group + 1:
            products[step - 1] = multiply(turned.pop(step - 1))
        if step < group:
            turned[step] = spread(step)
    for (block, seq), target in slots.items():
        place = seq % 2 * blocks + block
        send_ref[target, group * pair :, :] = back_scr[
            place * back_rows : place * back_rows + group * half, :
        ].astype(jnp.bfloat16)


def unpack_kernel(
    group, mask_ref, recv_ref, conv_ref, grad_ref, pair_scr, conv_buf, grad_buf, sems
):
    tokens, channels = conv_ref.shape[1:]
    rows = tokens // LANES
    pair = 2 * rows
    pitch = pair + PAD
    block_rows = BLK // LANES
    size = group * pair
    for source in range(recv_ref.shape[0]):
        whole = recv_ref[source, :size, :].astype(jnp.float32)
        for index in range(group):
            start = (source * group + index) * pitch
            pair_scr[start : start + pair, :] = whole[index * pair : (index + 1) * pair]
    copies = []
    for row in range(rows):
        span = pl.ds(row * LANES, LANES)
        keep = mask_ref[0, row // block_rows].astype(jnp.float32)
        conv_buf[span, :] = pair_scr[pl.ds(row, channels, stride=pitch), :].T.astype(jnp.bfloat16)
        copies.append(
            pltpu.make_async_copy(conv_buf.at[span, :], conv_ref.at[0, span, :], sems.at[2 * row])
        )
        copies[-1].start()
        grad_buf[span, :] = (
            pair_scr[pl.ds(rows + row, channels, stride=pitch), :].T * keep
        ).astype(jnp.bfloat16)
        copies.append(
            pltpu.make_async_copy(
                grad_buf.at[span, :], grad_ref.at[0, span, :], sems.at[2 * row + 1]
            )
        )
        copies[-1].start()
    for copy in copies:
        copy.wait()


def unpack_taps_kernel(group, own_ref, other_ref, taps_ref, scr, taps_buf, sems):
    tokens, channels = taps_ref.shape
    half = tokens // LANES // 2
    size = group * half
    side = lax.rem(lax.axis_index("dp"), 2)
    copies = []
    for place, ref in enumerate((own_ref, other_ref)):
        base = place * ref.shape[0] * size
        for source in range(ref.shape[0]):
            scr[base + source * size : base + (source + 1) * size, :] = ref[source].astype(
                jnp.float32
            )
        start = jnp.where(side == place, 0, half * LANES)
        for row in range(half):
            slot = place * half + row
            span = pl.ds(slot * LANES, LANES)
            taps_buf[span, :] = scr[pl.ds(base + row, channels, stride=half), :].T.astype(
                jnp.bfloat16
            )
            goal = pl.ds(pl.multiple_of(start + row * LANES, LANES), LANES)
            copies.append(
                pltpu.make_async_copy(taps_buf.at[span, :], taps_ref.at[goal, :], sems.at[slot])
            )
            copies[-1].start()
    for copy in copies:
        copy.wait()


VMEM = pl.BlockSpec(memory_space=pltpu.VMEM)
SMEM = pl.BlockSpec(memory_space=pltpu.SMEM)
HBM = pl.BlockSpec(memory_space=pltpu.HBM)
LIMIT = pltpu.CompilerParams(vmem_limit_bytes=48 * 1024 * 1024)


def per_device(signal, filter_raw, cotangent, block_mask):
    tokens, channels = filter_raw.shape
    blocks = lax.axis_size("seq")
    replicas = lax.axis_size("dp")
    count = blocks * replicas
    group = -(-channels // count)
    rows = tokens // LANES
    pair = 2 * rows
    own = rows // replicas
    half = rows // 2
    total = tokens * blocks
    coarse = total // LANES
    factor = 1.0 / (total * math.sqrt(total))
    everyone = ("seq", "dp")
    ring = [[block * replicas + seq for block, seq in slot_order(blocks, replicas)]]
    tables = [jnp.asarray(t) for t in make_tables(blocks, rows, replicas)]

    inputs = (signal, cotangent, filter_raw)
    packed = pl.pallas_call(
        functools.partial(pack_kernel, own, group, count),
        out_shape=pltpu.VMEM((count, group * (pair + own), LANES), jnp.bfloat16),
        in_specs=[SMEM, HBM, HBM, HBM],
        out_specs=VMEM,
        scratch_shapes=[
            pltpu.VMEM((tokens, channels), jnp.bfloat16),
            pltpu.VMEM((tokens, channels), jnp.bfloat16),
            pltpu.VMEM((own * LANES, channels), jnp.bfloat16),
            pltpu.VMEM(((count * group + 1) * (pair + PAD), LANES), jnp.float32),
            pltpu.VMEM(((count * group + 1) * own, LANES), jnp.float32),
            pltpu.SemaphoreType.DMA((3,)),
        ],
        compiler_params=LIMIT,
        name="pack",
    )(block_mask, *(pltpu.with_memory_space_constraint(x, pltpu.HBM) for x in inputs))
    received = lax.all_to_all(packed, everyone, split_axis=0, concat_axis=0, tiled=True, axis_index_groups=ring)
    results = pl.pallas_call(
        functools.partial(spectral_kernel, blocks, rows, replicas, group, factor),
        out_shape=jax.ShapeDtypeStruct((count, group * (pair + half), LANES), jnp.bfloat16),
        in_specs=[VMEM] * 9,
        out_specs=VMEM,
        scratch_shapes=[
            pltpu.VMEM(((count + 1) * (group * own + PAD), LANES), jnp.float32),
            pltpu.VMEM(((2 * blocks + 1) * (group * half + PAD), LANES), jnp.float32),
        ],
        compiler_params=LIMIT,
        name="spectral",
    )(received, *tables)
    returned = lax.all_to_all(results, everyone, split_axis=0, concat_axis=0, tiled=True, axis_index_groups=ring)
    own_taps = returned[:, group * pair :, :]
    other_taps = lax.ppermute(own_taps, "dp", [(i, i ^ 1) for i in range(replicas)])
    conv_out, signal_grad = pl.pallas_call(
        functools.partial(unpack_kernel, group),
        out_shape=[jax.ShapeDtypeStruct(signal.shape, jnp.bfloat16)] * 2,
        in_specs=[SMEM, VMEM],
        out_specs=[HBM, HBM],
        scratch_shapes=[
            pltpu.VMEM(((count * group + 1) * (pair + PAD), LANES), jnp.float32),
            pltpu.VMEM((tokens, channels), jnp.bfloat16),
            pltpu.VMEM((tokens, channels), jnp.bfloat16),
            pltpu.SemaphoreType.DMA((2 * rows,)),
        ],
        compiler_params=LIMIT,
        name="unpack",
    )(block_mask, returned)
    filter_grad = pl.pallas_call(
        functools.partial(unpack_taps_kernel, group),
        out_shape=jax.ShapeDtypeStruct(filter_raw.shape, jnp.bfloat16),
        in_specs=[VMEM, VMEM],
        out_specs=HBM,
        scratch_shapes=[
            pltpu.VMEM(((2 * count * group + 1) * half, LANES), jnp.float32),
            pltpu.VMEM((tokens, channels), jnp.bfloat16),
            pltpu.SemaphoreType.DMA((2 * half,)),
        ],
        compiler_params=LIMIT,
        name="unpack_taps",
    )(own_taps, other_taps)
    return conv_out, signal_grad, filter_grad


def solution(mesh):
    placed = (P("dp", "seq", None), P("seq", None), P("dp", "seq", None), P("dp", "seq"))
    return jax.shard_map(
        per_device,
        mesh=mesh,
        in_specs=placed,
        out_specs=(P("dp", "seq", None), P("dp", "seq", None), P("seq", None)),
        check_vma=False,
    )
```

```python
import functools
import math

import jax
import jax.numpy as jnp
import ml_dtypes
import numpy as np
from jax import lax
from jax.experimental import pallas as pl
from jax.experimental.pallas import tpu as pltpu
from jax.sharding import PartitionSpec as P

LANES = 128
BLK = 1024
PAD = 1
BF16 = ml_dtypes.bfloat16


def wave(product, period):
    angle = 2.0 * np.pi / period * (product % period)
    return np.cos(angle), np.sin(angle)


def slot_order(blocks, replicas):
    turns = [0] + list(range((blocks - 1) // 2, 0, -1))
    return [
        (2 * turn + odd, seq) for odd in range(2) for seq in range(replicas) for turn in turns
    ]


def make_tables(blocks, rows, replicas):
    coarse = blocks * rows
    freq = np.arange(coarse)
    lane = np.arange(LANES)
    own = rows // replicas
    half = rows // 2
    grid_j, grid_r = np.meshgrid(np.arange(blocks), np.arange(rows), indexing="ij")
    plain = grid_j * rows + grid_r
    cos_a, sin_a = wave((4 * freq[:, None] + 1) * np.arange(coarse)[None, :], 4 * coarse)
    first = np.zeros((2, 2, coarse, blocks, 2, rows))
    last = np.zeros((blocks, 2, rows, 2, 2, coarse))
    for which in range(2):
        first[which, 0, :, :, which, :] = cos_a[:, plain]
        first[which, 1, :, :, which, :] = -sin_a[:, plain]
        last[:, which, :, which, 0, :] = np.moveaxis(cos_a[:, plain], 0, 2)
        last[:, which, :, which, 1, :] = -np.moveaxis(sin_a[:, plain], 0, 2)
    starts = np.array([rows * block + own * seq for block, seq in slot_order(blocks, replicas)])
    taps = (np.arange(own)[:, None] + starts[None, :]).reshape(-1)
    first_taps = np.concatenate([cos_a[:, taps], -sin_a[:, taps]], axis=0)
    back = (
        np.arange(half)[:, None, None]
        + half * np.arange(2)[None, :, None]
        + rows * np.arange(blocks)[None, None, :]
    ).reshape(-1)
    last_taps = np.concatenate([cos_a[:, back], -sin_a[:, back]], axis=0).T
    twist_cos, twist_sin = wave((4 * freq[:, None] + 1) * lane[None, :], 4 * LANES * coarse)
    cos_l, sin_l = wave(lane[:, None] * lane[None, :], LANES)
    inner = np.block([[cos_l, -sin_l], [sin_l, cos_l]])
    inner_back = np.block([[cos_l, sin_l], [-sin_l, cos_l]])
    narrow = (
        first.reshape(4 * coarse, 2 * coarse),
        first_taps,
        inner,
        inner_back,
        last.reshape(2 * coarse, 4 * coarse),
        last_taps,
    )
    return tuple(t.astype(np.float32).astype(BF16) for t in narrow) + (
        twist_cos.astype(np.float32),
        twist_sin.astype(np.float32),
    )


def pack_kernel(
    own, group, count, mask_ref, signal_ref, grad_ref, filter_ref, send_ref,
    signal_buf, grad_buf, filter_buf, pair_scr, tap_scr, in_sems,
):
    tokens, channels = filter_ref.shape
    rows = tokens // LANES
    pair = 2 * rows
    pitch = pair + PAD
    block_rows = BLK // LANES
    parts = in_sems.shape[0] // 2
    part_rows = rows // parts
    start = pl.multiple_of(lax.axis_index("dp") * (own * LANES), own * LANES)
    filter_copy = pltpu.make_async_copy(
        filter_ref.at[pl.ds(start, own * LANES), :], filter_buf, in_sems.at[2 * parts]
    )
    copies = []
    for part in range(parts):
        span = pl.ds(part * part_rows * LANES, part_rows * LANES)
        copies.append(
            pltpu.make_async_copy(
                signal_ref.at[0, span, :], signal_buf.at[span, :], in_sems.at[2 * part]
            )
        )
        copies.append(
            pltpu.make_async_copy(
                grad_ref.at[0, span, :], grad_buf.at[span, :], in_sems.at[2 * part + 1]
            )
        )
    for copy in copies:
        copy.start()
    filter_copy.start()
    if group * count != channels:
        pair_scr[...] = jnp.zeros_like(pair_scr)
        tap_scr[...] = jnp.zeros_like(tap_scr)
    copies[0].wait()
    for row in range(rows):
        keep = mask_ref[0, row // block_rows].astype(jnp.float32)
        pair_scr[pl.ds(row, channels, stride=pitch), :] = (
            signal_buf[row * LANES : (row + 1) * LANES, :].astype(jnp.float32).T * keep
        )
    copies[1].wait()
    filter_copy.wait()
    for row in range(rows):
        pair_scr[pl.ds(rows + row, channels, stride=pitch), :] = (
            grad_buf[row * LANES : (row + 1) * LANES, :].astype(jnp.float32).T
        )
    for row in range(own):
        tap_scr[pl.ds(row, channels, stride=own), :] = (
            filter_buf[row * LANES : (row + 1) * LANES, :].astype(jnp.float32).T
        )
    for target in range(count):
        send_ref[target, : group * pair, :] = jnp.concatenate(
            [
                pair_scr[index * pitch : index * pitch + pair, :]
                for index in range(target * group, (target + 1) * group)
            ],
            axis=0,
        ).astype(jnp.bfloat16)
        send_ref[target, group * pair :, :] = tap_scr[
            target * group * own : (target + 1) * group * own, :
        ].astype(jnp.bfloat16)


def spectral_kernel(
    blocks, rows, replicas, group, factor,
    recv_ref, first_ref, first_taps_ref, inner_ref, inner_back_ref, last_ref, last_taps_ref,
    twist_cos_ref, twist_sin_ref, send_ref, tap_scr, back_scr,
):
    coarse = blocks * rows
    count = blocks * replicas
    pair = 2 * rows
    own = rows // replicas
    half = rows // 2
    slots = {place: slot for slot, place in enumerate(slot_order(blocks, replicas))}
    tap_rows = group * own + PAD
    back_rows = group * half + PAD
    for source in range(count):
        tap_scr[source * tap_rows : source * tap_rows + group * own, :] = recv_ref[
            source, group * pair :, :
        ].astype(jnp.float32)

    def dot(left, right):
        return jnp.dot(left, right, preferred_element_type=jnp.float32)

    def spread(index):
        offset = index * pair
        twist_cos = twist_cos_ref[...]
        twist_sin = twist_sin_ref[...]

        def turn(real, imag):
            return jnp.concatenate(
                [real * twist_cos + imag * twist_sin, imag * twist_cos - real * twist_sin], axis=1
            ).astype(jnp.bfloat16)

        taps = jnp.concatenate(
            [tap_scr[pl.ds(index * own + row, count, stride=tap_rows), :] for row in range(own)],
            axis=0,
        ).astype(jnp.bfloat16)
        wide_taps = dot(first_taps_ref[...], taps)
        data = jnp.concatenate(
            [
                jnp.concatenate(
                    [
                        recv_ref[slots[block, seq], pl.ds(offset, pair), :]
                        for block in range(blocks)
                    ],
                    axis=0,
                )
                for seq in range(replicas)
            ],
            axis=1,
        )
        wide = dot(first_ref[...], data)
        turned = [turn(wide_taps[:coarse], wide_taps[coarse:])]
        for seq in range(replicas):
            part = wide[:, seq * LANES : (seq + 1) * LANES]
            for which in range(2):
                base = 2 * which * coarse
                turned.append(
                    turn(part[base : base + coarse], part[base + coarse : base + 2 * coarse])
                )
        return jnp.concatenate(turned, axis=0)

    def multiply(turned):
        spectrum = dot(turned, inner_ref[...])

        def pick(place):
            piece = spectrum[place * coarse : (place + 1) * coarse]
            return piece[:, :LANES], piece[:, LANES:]

        filter_real, filter_imag = pick(0)
        products = []
        weight_real = weight_imag = None
        for seq in range(replicas):
            signal_real, signal_imag = pick(1 + 2 * seq)
            grad_real, grad_imag = pick(2 + 2 * seq)
            out = (
                signal_real * filter_real - signal_imag * filter_imag,
                signal_real * filter_imag + signal_imag * filter_real,
            )
            into = (
                grad_real * filter_real + grad_imag * filter_imag,
                grad_imag * filter_real - grad_real * filter_imag,
            )
            term_real = grad_real * signal_real + grad_imag * signal_imag
            term_imag = grad_imag * signal_real - grad_real * signal_imag
            weight_real = term_real if weight_real is None else weight_real + term_real
            weight_imag = term_imag if weight_imag is None else weight_imag + term_imag
            products.append(jnp.concatenate(out, axis=1).astype(jnp.bfloat16))
            products.append(jnp.concatenate(into, axis=1).astype(jnp.bfloat16))
        products.append(
            jnp.concatenate([weight_real, weight_imag], axis=1).astype(jnp.bfloat16)
        )
        return jnp.concatenate(products, axis=0)

    def narrow(products):
        inverted = dot(products, inner_back_ref[...])
        twist_cos = twist_cos_ref[...]
        twist_sin = twist_sin_ref[...]

        def turn_back(place):
            piece = inverted[place * coarse : (place + 1) * coarse]
            real, imag = piece[:, :LANES], piece[:, LANES:]
            return jnp.concatenate(
                [real * twist_cos - imag * twist_sin, imag * twist_cos + real * twist_sin], axis=0
            ).astype(jnp.bfloat16)

        columns = jnp.concatenate(
            [
                jnp.concatenate([turn_back(2 * seq), turn_back(2 * seq + 1)], axis=0)
                for seq in range(replicas)
            ],
            axis=1,
        )
        return columns, turn_back(2 * replicas)

    def finish(index, columns, weight_column):
        offset = index * pair
        result = (dot(last_ref[...], columns) * factor).astype(jnp.bfloat16)
        for seq in range(replicas):
            for block in range(blocks):
                send_ref[slots[block, seq], pl.ds(offset, pair), :] = result[
                    block * pair : (block + 1) * pair, seq * LANES : (seq + 1) * LANES
                ]
        weights = dot(last_taps_ref[...], weight_column) * factor
        for row in range(half):
            back_scr[pl.ds(index * half + row, 2 * blocks, stride=back_rows), :] = weights[
                row * 2 * blocks : (row + 1) * 2 * blocks
            ]

    turned, products, columns = {}, {}, {}
    for step in range(group + 3):
        if step >= 3:
            finish(step - 3, *columns.pop(step - 3))
        if 2 <= step < group + 2:
            columns[step - 2] = narrow(products.pop(step - 2))
        if 1 <= step < group + 1:
            products[step - 1] = multiply(turned.pop(step - 1))
        if step < group:
            turned[step] = spread(step)
    for (block, seq), target in slots.items():
        place = seq % 2 * blocks + block
        send_ref[target, group * pair :, :] = back_scr[
            place * back_rows : place * back_rows + group * half, :
        ].astype(jnp.bfloat16)


def place_taps(group, side, part_ref, taps_ref, scr, taps_buf, sem):
    tokens, channels = taps_ref.shape
    half = tokens // LANES // 2
    size = group * half
    for source in range(part_ref.shape[0]):
        scr[source * size : (source + 1) * size, :] = part_ref[source].astype(jnp.float32)
    for row in range(half):
        span = pl.ds(row * LANES, LANES)
        taps_buf[span, :] = scr[pl.ds(row, channels, stride=half), :].T.astype(jnp.bfloat16)
    goal = pl.ds(pl.multiple_of(side * (half * LANES), half * LANES), half * LANES)
    copy = pltpu.make_async_copy(taps_buf, taps_ref.at[goal, :], sem)
    copy.start()
    return copy


def unpack_kernel(
    group, mask_ref, recv_ref, conv_ref, grad_ref, taps_ref, pair_scr, conv_buf, grad_buf,
    tap_scr, taps_buf, sems, tap_sem,
):
    tokens, channels = conv_ref.shape[1:]
    rows = tokens // LANES
    pair = 2 * rows
    pitch = pair + PAD
    block_rows = BLK // LANES
    size = group * pair
    for source in range(recv_ref.shape[0]):
        whole = recv_ref[source, :size, :].astype(jnp.float32)
        for index in range(group):
            start = (source * group + index) * pitch
            pair_scr[start : start + pair, :] = whole[index * pair : (index + 1) * pair]
    copies = []
    for row in range(rows):
        span = pl.ds(row * LANES, LANES)
        keep = mask_ref[0, row // block_rows].astype(jnp.float32)
        conv_buf[span, :] = pair_scr[pl.ds(row, channels, stride=pitch), :].T.astype(jnp.bfloat16)
        copies.append(
            pltpu.make_async_copy(conv_buf.at[span, :], conv_ref.at[0, span, :], sems.at[2 * row])
        )
        copies[-1].start()
        grad_buf[span, :] = (
            pair_scr[pl.ds(rows + row, channels, stride=pitch), :].T * keep
        ).astype(jnp.bfloat16)
        copies.append(
            pltpu.make_async_copy(
                grad_buf.at[span, :], grad_ref.at[0, span, :], sems.at[2 * row + 1]
            )
        )
        copies[-1].start()
    side = lax.rem(lax.axis_index("dp"), 2)
    copies.append(
        place_taps(
            group, side, recv_ref.at[:, pl.ds(size, group * rows // 2), :], taps_ref,
            tap_scr, taps_buf, tap_sem,
        )
    )
    for copy in copies:
        copy.wait()


def unpack_taps_kernel(group, other_ref, kept_ref, taps_ref, scr, taps_buf, sem):
    side = 1 - lax.rem(lax.axis_index("dp"), 2)
    place_taps(group, side, other_ref, taps_ref, scr, taps_buf, sem).wait()


VMEM = pl.BlockSpec(memory_space=pltpu.VMEM)
SMEM = pl.BlockSpec(memory_space=pltpu.SMEM)
HBM = pl.BlockSpec(memory_space=pltpu.HBM)
LIMIT = pltpu.CompilerParams(vmem_limit_bytes=48 * 1024 * 1024)


def per_device(signal, filter_raw, cotangent, block_mask):
    tokens, channels = filter_raw.shape
    blocks = lax.axis_size("seq")
    replicas = lax.axis_size("dp")
    count = blocks * replicas
    group = -(-channels // count)
    rows = tokens // LANES
    pair = 2 * rows
    own = rows // replicas
    half = rows // 2
    total = tokens * blocks
    coarse = total // LANES
    factor = 1.0 / (total * math.sqrt(total))
    everyone = ("seq", "dp")
    ring = [[block * replicas + seq for block, seq in slot_order(blocks, replicas)]]
    tables = [jnp.asarray(t) for t in make_tables(blocks, rows, replicas)]

    inputs = (signal, cotangent, filter_raw)
    packed = pl.pallas_call(
        functools.partial(pack_kernel, own, group, count),
        out_shape=pltpu.VMEM((count, group * (pair + own), LANES), jnp.bfloat16),
        in_specs=[SMEM, HBM, HBM, HBM],
        out_specs=VMEM,
        scratch_shapes=[
            pltpu.VMEM((tokens, channels), jnp.bfloat16),
            pltpu.VMEM((tokens, channels), jnp.bfloat16),
            pltpu.VMEM((own * LANES, channels), jnp.bfloat16),
            pltpu.VMEM(((count * group + 1) * (pair + PAD), LANES), jnp.float32),
            pltpu.VMEM(((count * group + 1) * own, LANES), jnp.float32),
            pltpu.SemaphoreType.DMA((3,)),
        ],
        compiler_params=LIMIT,
        name="pack",
    )(block_mask, *(pltpu.with_memory_space_constraint(x, pltpu.HBM) for x in inputs))
    received = lax.all_to_all(packed, everyone, split_axis=0, concat_axis=0, tiled=True, axis_index_groups=ring)
    results = pl.pallas_call(
        functools.partial(spectral_kernel, blocks, rows, replicas, group, factor),
        out_shape=jax.ShapeDtypeStruct((count, group * (pair + half), LANES), jnp.bfloat16),
        in_specs=[VMEM] * 9,
        out_specs=VMEM,
        scratch_shapes=[
            pltpu.VMEM(((count + 1) * (group * own + PAD), LANES), jnp.float32),
            pltpu.VMEM(((2 * blocks + 1) * (group * half + PAD), LANES), jnp.float32),
        ],
        compiler_params=LIMIT,
        name="spectral",
    )(received, *tables)
    returned = lax.all_to_all(results, everyone, split_axis=0, concat_axis=0, tiled=True, axis_index_groups=ring)
    own_taps = returned[:, group * pair :, :]
    other_taps = lax.ppermute(own_taps, "dp", [(i, i ^ 1) for i in range(replicas)])
    tap_scratch = [
        pltpu.VMEM(((count * group + 1) * half, LANES), jnp.float32),
        pltpu.VMEM((half * LANES, channels), jnp.bfloat16),
    ]
    conv_out, signal_grad, half_grad = pl.pallas_call(
        functools.partial(unpack_kernel, group),
        out_shape=[jax.ShapeDtypeStruct(signal.shape, jnp.bfloat16)] * 2
        + [jax.ShapeDtypeStruct(filter_raw.shape, jnp.bfloat16)],
        in_specs=[SMEM, VMEM],
        out_specs=[HBM, HBM, HBM],
        scratch_shapes=[
            pltpu.VMEM(((count * group + 1) * (pair + PAD), LANES), jnp.float32),
            pltpu.VMEM((tokens, channels), jnp.bfloat16),
            pltpu.VMEM((tokens, channels), jnp.bfloat16),
            *tap_scratch,
            pltpu.SemaphoreType.DMA((2 * rows,)),
            pltpu.SemaphoreType.DMA,
        ],
        compiler_params=LIMIT,
        name="unpack",
    )(block_mask, returned)
    filter_grad = pl.pallas_call(
        functools.partial(unpack_taps_kernel, group),
        out_shape=jax.ShapeDtypeStruct(filter_raw.shape, jnp.bfloat16),
        in_specs=[VMEM, HBM],
        out_specs=HBM,
        scratch_shapes=[*tap_scratch, pltpu.SemaphoreType.DMA],
        input_output_aliases={1: 0},
        compiler_params=LIMIT,
        name="unpack_taps",
    )(other_taps, half_grad)
    return conv_out, signal_grad, filter_grad


def solution(mesh):
    placed = (P("dp", "seq", None), P("seq", None), P("dp", "seq", None), P("dp", "seq"))
    return jax.shard_map(
        per_device,
        mesh=mesh,
        in_specs=placed,
        out_specs=(P("dp", "seq", None), P("dp", "seq", None), P("seq", None)),
        check_vma=False,
    )
```
